128 devices in a mesh: ty: 8 (over x, core), tx: 16 (over z, y).
Axes of the slice: x: 4, y: 4, z: 4, core: 2. Of those that a mesh axis runs over, the one named last changes fastest.
Arguments:
- beam_depth: float32 [8192, 512], P(('ty', 'tx')), may hold values from -6 to 6
- backscatter: float32 [8192, 512], P(('ty', 'tx')), may hold values from -6 to 6
- grazing: float32 [8192, 512], P(('ty', 'tx')), may hold values from -6 to 6
- quality: float32 [8192, 512], P(('ty', 'tx')), may hold values from 0.25 to 2
- beam_valid: int32 [8192, 512], P(('ty', 'tx')), may hold values 0 or 1
- beam_row: int32 [8192, 512], P(('ty', 'tx')), may hold values from 0 to 63
- beam_col: int32 [8192, 512], P(('ty', 'tx')), may hold values from 0 to 63
- tidal_zone: int32 [8192], P(('ty', 'tx')), may hold values from 0 to 63
- ping_tile: int32 [8192], P(('ty', 'tx')), may hold values from 0 to 127, as said below
- tide_offsets: float32 [64], replicated, may hold values from -1 to 1
Outputs:
- gridded: float32 [8, 512, 1024], P(None, 'ty', 'tx')
The draws below stay inside these ranges and needn't reach their ends.
Inputs may be any that keep to these rules, and one draw needn't show every extreme that they name: `ping_tile`: tile t is the tile in row t // 16 and column t % 16. In each aligned block of 64 pings no tile is named more than 2 times, and one tile is named exactly 2 times in every block.
All inputs are finite; a program needn't handle non-finite values. No bound on the sum of `beam_valid` on one device may be relied on, other than what follows from the above.
Results may differ from the reference program's by a relative error of at most 0.000073.
Values sent between devices are 32-bit elements; how exact they have to be, the bound alone decides.
No kernel may reach another device: no remote copies, remote signals or barrier semaphores. Data moves between devices by JAX's collectives and lax.ppermute only.
A program may use at most 64 MiB of HBM per device.

```python
import math
import jax
import jax.numpy as jnp
from jax import lax

BEAMS = 512
CHANNELS = 8
MARGIN = 7
ZONES = 64
TILE = 64
PING_DEV = 64
PINGS = 8192
NY = 512
NX = 1024
N_TY = 8
N_TX = 16


def draw_ping_tile(key, part):
    key = jax.random.fold_in(key, 11)
    tile_count = N_TY * N_TX
    capacity = 4 * PING_DEV // tile_count
    hottest = jax.random.randint(jax.random.fold_in(key, 1), (), 0, tile_count).astype(jnp.int32)

    def one_block(block_index):
        block_key = jax.random.fold_in(key, block_index + 2)
        slot_pool = jax.random.permutation(jax.random.fold_in(block_key, 0), (tile_count - 1) * capacity).astype(jnp.int32)
        others = slot_pool[:PING_DEV - capacity] // capacity
        others = others + (others >= hottest).astype(jnp.int32)
        names = jnp.concatenate([jnp.zeros((capacity,), jnp.int32) + hottest, others.astype(jnp.int32)])
        order = jax.random.permutation(jax.random.fold_in(block_key, 1), PING_DEV).astype(jnp.int32)
        return names[order]
    return jax.vmap(one_block)(jnp.arange(tile_count, dtype=jnp.int32)).reshape(-1).astype(jnp.int32)


def touch_ends(result, rng, smallest, largest):
    place = [jax.random.randint(jax.random.fold_in(rng, axis), (), 0, length) for axis, length in enumerate(result.shape)]
    longest = result.shape.index(max(result.shape))
    neighbour = place[:longest] + [(place[longest] + 1) % result.shape[longest]] + place[longest + 1:]
    return result.at[tuple(place)].set(smallest).at[tuple(neighbour)].set(largest)


def block_levels(stream_key, shape, shards, smallest, largest):
    def one(dim, blocks):
        heights = jax.random.uniform(jax.random.fold_in(jax.random.fold_in(stream_key, 6), dim), (blocks,), jnp.float32, smallest / len(shards), largest / len(shards))
        return jnp.repeat(jnp.exp(heights), shape[dim] // blocks).reshape((-1,) + (1,) * (len(shape) - dim - 1))

    factor_of = one(*shards[0])
    for cut in shards[1:]:
        factor_of = factor_of * one(*cut)
    return factor_of


def gaussian(own_key, extent, spread, limit, shards=(), kind=jnp.bfloat16):
    entries = jax.random.normal(own_key, extent, jnp.float32) * spread
    if len(shards) > 0:
        entries = block_levels(own_key, extent, shards, -0.22, 0.18) * entries
    return jnp.clip(entries, min=-limit, max=limit).astype(kind)


def setup_inputs(seed: int = 0) -> dict:
    arg_keys = jax.random.split(jax.random.key(seed), 11)
    beam_depth = gaussian(arg_keys[0], (PINGS, BEAMS), 1.0, 6.0, ((0, 128),), jnp.float32)
    backscatter = gaussian(arg_keys[1], (PINGS, BEAMS), 1.0, 6.0, ((0, 128),), jnp.float32)
    grazing = gaussian(arg_keys[2], (PINGS, BEAMS), 1.0, 6.0, ((0, 128),), jnp.float32)
    quality = jnp.clip(jnp.exp(math.log(2.0) - 2.0794415 * jax.random.uniform(arg_keys[3], (PINGS, BEAMS), jnp.float32) ** block_levels(arg_keys[3], (PINGS, BEAMS), ((0, 128),), -0.2, 0.2)), 0.25, 2.0)
    beam_valid = touch_ends((jax.random.randint(arg_keys[4], (PINGS, BEAMS), 0, 8) < 7).astype(jnp.int32), jax.random.fold_in(arg_keys[4], 1), 0, 1)
    beam_row = touch_ends(jax.random.randint(arg_keys[5], (PINGS, BEAMS), 0, TILE), jax.random.fold_in(arg_keys[5], 1), 0, TILE - 1).astype(jnp.int32)
    beam_col = touch_ends(jax.random.randint(arg_keys[6], (PINGS, BEAMS), 0, TILE), jax.random.fold_in(arg_keys[6], 1), 0, TILE - 1).astype(jnp.int32)
    tidal_zone = touch_ends(jax.random.randint(arg_keys[7], (PINGS,), 0, ZONES), jax.random.fold_in(arg_keys[7], 1), 0, ZONES - 1).astype(jnp.int32)
    ping_tile = draw_ping_tile(jax.random.fold_in(arg_keys[10], 71), 0)
    tide_offsets = jnp.clip(jax.random.uniform(arg_keys[9], (ZONES,), jnp.float32, -1.0, 1.0), -1.0, 1.0)
    return {"beam_depth": beam_depth, "backscatter": backscatter, "grazing": grazing, "quality": quality, "beam_valid": beam_valid, "beam_row": beam_row, "beam_col": beam_col, "tidal_zone": tidal_zone, "ping_tile": ping_tile, "tide_offsets": tide_offsets}


gauss_sigma = 2.5


def gaussian_taps():
    positions = jnp.arange(-MARGIN, MARGIN + 1).astype(jnp.float32)
    profile = jnp.exp(-0.5 * (positions / gauss_sigma) * (positions / gauss_sigma))
    return profile / jnp.sum(profile)


def statistics(height, backscatter, grazing, weight):
    return [weight, weight * height, weight * height * height, weight * backscatter,
            weight * backscatter * backscatter, weight * height * backscatter,
            weight * grazing, weight * grazing * grazing]


def smooth(field, which_axis, kernel_taps):
    length = field.shape[which_axis]
    widths = [(0, 0), (0, 0), (0, 0)]
    widths[which_axis] = (MARGIN, MARGIN)
    padded = jnp.pad(field, widths)
    total = jnp.zeros_like(field)
    for shift_index in range(2 * MARGIN + 1):
        total = total + kernel_taps[shift_index] * lax.slice_in_dim(padded, shift_index, shift_index + length, axis=which_axis)
    return total


def reference(beam_depth, backscatter, grazing, quality, beam_valid, beam_row, beam_col, tidal_zone, ping_tile, tide_offsets):
    height = tide_offsets[tidal_zone][:, None] - beam_depth
    weight = quality * beam_valid.astype(jnp.float32)
    stacked = jnp.stack(statistics(height, backscatter, grazing, weight), 0).reshape(CHANNELS, -1)
    tile_row = ping_tile // N_TX
    tile_col = ping_tile % N_TX
    wide_cols = NX + 2 * MARGIN
    global_row = tile_row[:, None] * TILE + beam_row + MARGIN
    global_col = tile_col[:, None] * TILE + beam_col + MARGIN
    flat_index = (global_row * wide_cols + global_col).reshape(-1).astype(jnp.int32)
    deposit = jnp.zeros((CHANNELS, (NY + 2 * MARGIN) * wide_cols), jnp.float32).at[:, flat_index].add(stacked)
    deposit = deposit.reshape(CHANNELS, NY + 2 * MARGIN, wide_cols)
    kernel_taps = gaussian_taps()
    smoothed = smooth(smooth(deposit, 1, kernel_taps), 2, kernel_taps)
    inner = smoothed[:, MARGIN:MARGIN + NY, MARGIN:MARGIN + NX]
    return inner / (1.0 + inner[0])[None]
```

```python
import functools
import math

import jax
import jax.numpy as jnp
from jax import lax
from jax.experimental import pallas as pl
from jax.experimental.pallas import tpu as pltpu
from jax.sharding import PartitionSpec as P

F32 = jnp.float32
BF16 = jnp.bfloat16
BEAMS = 512
CHANNELS = 8
MARGIN = 7
TILE = 64
FIELDS = 5
LANES = 128
GROUPS = BEAMS // LANES
RANKS = 2
BATCH = 8
SIGMA = 2.5
VMEM = pltpu.CompilerParams(vmem_limit_bytes=40 * 2**20)

_profile = [math.exp(-j * j / (2 * SIGMA * SIGMA)) for j in range(-MARGIN, MARGIN + 1)]
TAPS = [value / sum(_profile) for value in _profile]


def vmem():
    return pl.BlockSpec(memory_space=pltpu.VMEM)


def smem():
    return pl.BlockSpec(memory_space=pltpu.SMEM)


def pack_kernel(tile, zone, tide, depth, back, graz, quality, valid, row, col, out, seen):
    pings = depth.shape[0]
    slots = out.shape[0]

    def clear(i, _):
        seen[i] = 0
        return 0

    lax.fori_loop(0, slots // RANKS, clear, 0, unroll=8)

    def empty(i, _):
        out[i, FIELDS - 1] = jnp.full((GROUPS, LANES), -1.0, F32)
        return 0

    lax.fori_loop(0, slots, empty, 0, unroll=8)

    def place(p, _):
        target = tile[p]
        rank = seen[target]
        seen[target] = rank + 1
        slot = target * RANKS + rank
        offset = tide[zone[p]]
        here = pl.ds(p, 1)
        fields = (
            offset - depth[here, :],
            back[here, :],
            graz[here, :],
            quality[here, :] * valid[here, :].astype(F32),
            (row[here, :] * TILE + col[here, :]).astype(F32),
        )
        for f, values in enumerate(fields):
            for j in range(GROUPS):
                out[slot, f, pl.ds(j, 1), :] = values[:, j * LANES : (j + 1) * LANES]
        return 0

    lax.fori_loop(0, pings, place, 0, unroll=4)


def both(rows):
    return jnp.concatenate([rows, rows], 0).astype(BF16)


def factors(x, slot, spots):
    sub = lax.broadcasted_iota(jnp.int32, (8, LANES), 0)
    zero = jnp.zeros((16, LANES), BF16)
    one = jnp.ones((16, LANES), BF16)
    left, right = [], []
    for j in range(GROUPS):
        height, back, graz, weight, cell = (
            jnp.broadcast_to(x[slot, f, pl.ds(j, 1), :], (8, LANES)) for f in range(FIELDS)
        )
        first = jnp.where(
            (sub == 1) | (sub == 2) | (sub == 5),
            height,
            jnp.where((sub == 3) | (sub == 4), back, jnp.where(sub >= 6, graz, 1.0)),
        )
        second = jnp.where(
            sub == 2,
            height,
            jnp.where((sub == 4) | (sub == 5), back, jnp.where(sub == 7, graz, 1.0)),
        )
        stats = weight * first * second
        high = stats.astype(BF16).astype(F32)
        halves = jnp.concatenate([high, stats - high], 0).astype(BF16)
        coarse = jnp.floor(cell * (1.0 / 256.0))
        fine = both(cell - 256.0 * coarse)
        coarse = both(coarse)
        left.append(
            jnp.concatenate(
                [jnp.where(coarse == jnp.asarray(r, BF16), halves, zero) for r in range(16)], 0
            )
        )
        right.append(jnp.concatenate([jnp.where(fine == s, one, zero) for s in spots], 0))
    return jnp.concatenate(left, 1), jnp.concatenate(right, 1)


def deposit_kernel(first_cell, x, out, low, high, acc, order):
    slots = x.shape[0]

    def note(s, carry):
        count, gap = carry
        filled = first_cell[s] >= 0
        order[count] = s
        return count + filled.astype(jnp.int32), jnp.where(filled, gap, s)

    count, gap = lax.fori_loop(0, slots, note, (jnp.int32(0), jnp.int32(0)), unroll=8)
    for u in range(BATCH):
        order[count + u] = gap

    acc[...] = jnp.zeros_like(acc)
    base = lax.broadcasted_iota(jnp.int32, (16, LANES), 0)
    spots = [(base + 16 * i).astype(F32).astype(BF16) for i in range(16)]

    def step(t, _):
        pairs = [factors(x, order[t * BATCH + u], spots) for u in range(BATCH)]
        left = jnp.concatenate([a for a, _ in pairs], 1)
        right = jnp.concatenate([b for _, b in pairs], 1)
        part = lax.dot_general(
            left, right, (((1,), (1,)), ((), ())), preferred_element_type=F32
        )
        acc[0] += part[:, :LANES]
        acc[1] += part[:, LANES:]
        return 0

    lax.fori_loop(0, (count + BATCH - 1) // BATCH, step, 0)
    for ch in range(CHANNELS):
        for half in range(2):
            rows = acc[half, pl.ds(ch, 16, stride=16), :] + acc[half, pl.ds(ch + 8, 16, stride=16), :]
            for q in range(2):
                out[ch, pl.ds(2 * half + q, 16, stride=4), 0:TILE] = rows[:, q * TILE : (q + 1) * TILE]
        low[ch] = out[ch, 0:8, 0:TILE]
        high[ch] = out[ch, TILE - 8 : TILE, 0:TILE]


def smoothed_rows(ext, ch):
    total = None
    for j in range(2 * MARGIN + 1):
        term = TAPS[j] * ext[ch, pl.ds(1 + j, TILE), :]
        total = term if total is None else total + term
    return total


def extend(ext, before, own, after):
    for ch in range(CHANNELS):
        ext[ch, 0:8, :] = before[ch]
        ext[ch, 8 : 8 + TILE, :] = own[ch, :, 0:TILE]
        ext[ch, 8 + TILE : 16 + TILE, :] = after[ch]


def rows_kernel(before, own, after, out, low, high, ext):
    extend(ext, before, own, after)
    for ch in range(CHANNELS):
        turned = smoothed_rows(ext, ch).T
        out[ch] = turned
        low[ch] = turned[0:8]
        high[ch] = turned[TILE - 8 : TILE]


def columns_kernel(before, own, after, out, ext):
    extend(ext, before, own, after)
    scale = None
    for ch in range(CHANNELS):
        total = smoothed_rows(ext, ch)
        if ch == 0:
            scale = 1.0 + total
        out[ch] = (total / scale).T


def shift(x, axis, step):
    count = lax.axis_size(axis)
    return lax.ppermute(
        x, axis, [(i, i + step) for i in range(count) if 0 <= i + step < count]
    )


def shards(depth, back, graz, quality, valid, row, col, zone, tile, tide):
    devices = lax.axis_size("ty") * lax.axis_size("tx")
    slots = devices * RANKS
    shape = jax.ShapeDtypeStruct
    packed = pl.pallas_call(
        pack_kernel,
        out_shape=shape((slots, FIELDS, GROUPS, LANES), F32),
        in_specs=[smem()] * 3 + [vmem()] * 7,
        out_specs=vmem(),
        scratch_shapes=[pltpu.SMEM((devices,), jnp.int32)],
        compiler_params=VMEM,
        name="pack",
    )(tile, zone, tide, depth, back, graz, quality, valid, row, col)
    arrived = lax.all_to_all(packed, ("ty", "tx"), split_axis=0, concat_axis=0, tiled=True)
    first_cell = arrived[:, FIELDS - 1, 0, 0].astype(jnp.int32)
    rim = shape((CHANNELS, 8, TILE), F32)
    deposit, low, high = pl.pallas_call(
        deposit_kernel,
        out_shape=(shape((CHANNELS, TILE, LANES), F32), rim, rim),
        in_specs=[smem(), vmem()],
        out_specs=(vmem(),) * 3,
        scratch_shapes=[
            pltpu.VMEM((2, 256, LANES), F32),
            pltpu.SMEM((slots + BATCH,), jnp.int32),
        ],
        compiler_params=VMEM,
        name="deposit",
    )(first_cell, arrived)
    rows, low, high = pl.pallas_call(
        rows_kernel,
        out_shape=(shape((CHANNELS, TILE, TILE), F32), rim, rim),
        in_specs=[vmem()] * 3,
        out_specs=(vmem(),) * 3,
        scratch_shapes=[pltpu.VMEM((CHANNELS, TILE + 16, TILE), F32)],
        compiler_params=VMEM,
        name="rows",
    )(shift(high, "ty", 1), deposit, shift(low, "ty", -1))
    return pl.pallas_call(
        columns_kernel,
        out_shape=shape((CHANNELS, TILE, TILE), F32),
        in_specs=[vmem()] * 3,
        out_specs=vmem(),
        scratch_shapes=[pltpu.VMEM((CHANNELS, TILE + 16, TILE), F32)],
        compiler_params=VMEM,
        name="columns",
    )(shift(high, "tx", 1), rows, shift(low, "tx", -1))


def solution(mesh):
    pings = P(("ty", "tx"))
    return jax.shard_map(
        shards,
        mesh=mesh,
        in_specs=(pings,) * 9 + (P(),),
        out_specs=P(None, "ty", "tx"),
        check_vma=False,
    )
```

```python
import functools
import math

import jax
import jax.numpy as jnp
from jax import lax
from jax.experimental import pallas as pl
from jax.experimental.pallas import tpu as pltpu
from jax.sharding import PartitionSpec as P

F32 = jnp.float32
BF16 = jnp.bfloat16
BEAMS = 512
CHANNELS = 8
MARGIN = 7
TILE = 64
FIELDS = 5
LANES = 128
GROUPS = BEAMS // LANES
RANKS = 2
BATCH = 16
SIGMA = 2.5
VMEM = pltpu.CompilerParams(vmem_limit_bytes=40 * 2**20)

_profile = [math.exp(-j * j / (2 * SIGMA * SIGMA)) for j in range(-MARGIN, MARGIN + 1)]
TAPS = [value / sum(_profile) for value in _profile]


def vmem():
    return pl.BlockSpec(memory_space=pltpu.VMEM)


def pack_kernel(tile_h, zone_h, tide_h, depth_h, back_h, graz_h, quality_h, valid_h, row_h, col_h, out,
                tile, zone, tide, depth, back, graz, quality, valid, row, col, seen, sems):
    pings = depth.shape[0]
    slots = out.shape[0]
    copies = [
        pltpu.make_async_copy(source, target, sems.at[i])
        for i, (source, target) in enumerate(
            (
                (tile_h, tile),
                (zone_h, zone),
                (tide_h, tide),
                (depth_h, depth),
                (back_h, back),
                (graz_h, graz),
                (quality_h, quality),
                (valid_h, valid),
                (row_h, row),
                (col_h, col),
            )
        )
    ]
    for copy in copies:
        copy.start()

    def clear(i, _):
        seen[i] = 0
        return 0

    lax.fori_loop(0, slots // RANKS, clear, 0, unroll=8)

    def empty(i, _):
        out[i, FIELDS - 1] = jnp.full((GROUPS, LANES), -1.0, F32)
        return 0

    lax.fori_loop(0, slots, empty, 0, unroll=8)
    for copy in copies:
        copy.wait()

    def place(p, _):
        target = tile[p]
        rank = seen[target]
        seen[target] = rank + 1
        down, across = lax.shift_right_logical(target, 4), target & 15
        chip = lax.shift_right_logical(down, 1) * 16 + across
        slot = chip * 4 + (down & 1) * 2 + rank
        offset = tide[zone[p]]
        here = pl.ds(p, 1)
        fields = (
            offset - depth[here, :],
            back[here, :],
            graz[here, :],
            quality[here, :] * valid[here, :].astype(F32),
            (row[here, :] * TILE + col[here, :]).astype(F32),
        )
        for f, values in enumerate(fields):
            for j in range(GROUPS):
                out[slot, f, pl.ds(j, 1), :] = values[:, j * LANES : (j + 1) * LANES]
        return 0

    lax.fori_loop(0, pings, place, 0, unroll=4)


def both(rows):
    return jnp.concatenate([rows, rows], 0).astype(BF16)


def factors(x, slot, spots):
    sub = lax.broadcasted_iota(jnp.int32, (8, LANES), 0)
    zero = jnp.zeros((16, LANES), BF16)
    one = jnp.ones((16, LANES), BF16)
    left, right = [], []
    for j in range(GROUPS):
        height, back, graz, weight, cell = (
            jnp.broadcast_to(x[slot, f, pl.ds(j, 1), :], (8, LANES)) for f in range(FIELDS)
        )
        first = jnp.where(
            (sub == 1) | (sub == 2) | (sub == 5),
            height,
            jnp.where((sub == 3) | (sub == 4), back, jnp.where(sub >= 6, graz, 1.0)),
        )
        second = jnp.where(
            sub == 2,
            height,
            jnp.where((sub == 4) | (sub == 5), back, jnp.where(sub == 7, graz, 1.0)),
        )
        stats = weight * first * second
        high = stats.astype(BF16).astype(F32)
        halves = jnp.concatenate([high, stats - high], 0).astype(BF16)
        coarse = jnp.floor(cell * (1.0 / 256.0))
        fine = both(cell - 256.0 * coarse)
        coarse = both(coarse)
        left.append(
            jnp.concatenate(
                [jnp.where(coarse == jnp.asarray(r, BF16), halves, zero) for r in range(16)], 0
            )
        )
        right.append(jnp.concatenate([jnp.where(fine == s, one, zero) for s in spots], 0))
    return jnp.concatenate(left, 1), jnp.concatenate(right, 1)


def deposit_kernel(x, mine, mates, acc, part, heads, flags_v, flags, upper, lower, sem):
    slots = x.shape[0]
    core = lax.axis_index("ty") % 2

    def head(s, _):
        heads[pl.ds(s, 1), :] = x[s, FIELDS - 1, pl.ds(0, 1), :]
        return 0

    lax.fori_loop(0, slots, head, 0, unroll=16)
    pick = jnp.where(lax.broadcasted_iota(jnp.int32, (8, LANES), 1) == 0, 1.0, 0.0)
    filled = jnp.where(heads[...] >= 0.0, 1.0, 0.0)
    flags_v[...] = lax.dot_general(
        pick.astype(BF16), filled.astype(BF16), (((1,), (1,)), ((), ())),
        preferred_element_type=F32,
    ).astype(jnp.int32)
    copy = pltpu.make_async_copy(flags_v, flags, sem)
    copy.start()
    acc[...] = jnp.zeros_like(acc)
    copy.wait()

    def note(q, carry):
        counts = list(carry[:2])
        gaps = list(carry[2:])
        for side, order in enumerate((upper, lower)):
            for rank in range(RANKS):
                s = q * 4 + side * 2 + rank
                full = flags[0, s]
                order[counts[side]] = s
                counts[side] = counts[side] + full
                gaps[side] = jnp.where(full > 0, gaps[side], s)
        return (*counts, *gaps)

    zero = jnp.int32(0)
    counts = lax.fori_loop(0, slots // 4, note, (zero, zero, zero, zero), unroll=4)
    base = lax.broadcasted_iota(jnp.int32, (16, LANES), 0)
    spots = [(base + 16 * i).astype(F32).astype(BF16) for i in range(16)]
    for side, order in enumerate((upper, lower)):
        for u in range(BATCH):
            order[counts[side] + u] = counts[2 + side]

    def step(t, _, side, order):
        pairs = [factors(x, order[t * BATCH + u], spots) for u in range(BATCH)]
        left = jnp.concatenate([a for a, _ in pairs], 1)
        right = jnp.concatenate([b for _, b in pairs], 1)
        total = lax.dot_general(
            left, right, (((1,), (1,)), ((), ())), preferred_element_type=F32
        )
        acc[side, 0] += total[:, :LANES]
        acc[side, 1] += total[:, LANES:]
        return 0

    for side, order in enumerate((upper, lower)):
        turns = (counts[side] + BATCH - 1) // BATCH
        lax.fori_loop(0, turns, functools.partial(step, side=side, order=order), 0)
        for ch in range(CHANNELS):
            for half in range(2):
                rows = acc[side, half, pl.ds(ch, 16, stride=16), :]
                rows += acc[side, half, pl.ds(ch + 8, 16, stride=16), :]
                for q in range(2):
                    part[ch, pl.ds(TILE * side + 2 * half + q, 16, stride=4), 0:TILE] = rows[
                        :, q * TILE : (q + 1) * TILE
                    ]
    own = pl.ds(pl.multiple_of(core * (TILE - 8), 8), TILE + 8)
    other = pl.ds(pl.multiple_of((1 - core) * (TILE - 8), 8), TILE + 8)
    for ch in range(CHANNELS):
        mine[ch] = part[ch, own, 0:TILE]
        mates[ch] = part[ch, other, 0:TILE]


def join_kernel(mine, mates, total, rim):
    core = lax.axis_index("ty") % 2
    for ch in range(CHANNELS):
        total[ch] = mine[ch] + mates[ch]
        rim[ch] = total[ch, pl.ds(pl.multiple_of(core * TILE, 8), 8), :]


def smoothed(ext, ch):
    total = None
    for j in range(2 * MARGIN + 1):
        term = TAPS[j] * ext[ch, pl.ds(1 + j, TILE), :]
        total = term if total is None else total + term
    return total


def rows_kernel(window, rim, out, near, far, ext):
    core = lax.axis_index("ty") % 2
    odd = lax.axis_index("tx") % 2
    inside = pl.ds(pl.multiple_of(8 - core * 8, 8), TILE + 8)
    outside = pl.ds(pl.multiple_of(core * (TILE + 8), 8), 8)
    for ch in range(CHANNELS):
        ext[ch, inside, :] = window[ch]
        ext[ch, outside, :] = rim[ch]
    for ch in range(CHANNELS):
        out[ch] = smoothed(ext, ch).T
        near[ch] = out[ch, pl.ds(pl.multiple_of((1 - odd) * (TILE - 8), 8), 8), :]
        far[ch] = out[ch, pl.ds(pl.multiple_of(odd * (TILE - 8), 8), 8), :]


def columns_kernel(own, near, far, out, ext):
    odd = lax.axis_index("tx") % 2
    near_rows = pl.ds(pl.multiple_of((1 - odd) * (TILE + 8), 8), 8)
    far_rows = pl.ds(pl.multiple_of(odd * (TILE + 8), 8), 8)
    for ch in range(CHANNELS):
        ext[ch, 8 : 8 + TILE, :] = own[ch]
        ext[ch, near_rows, :] = near[ch]
        ext[ch, far_rows, :] = far[ch]
    scale = None
    for ch in range(CHANNELS):
        total = smoothed(ext, ch)
        if ch == 0:
            scale = 1.0 + total
        out[ch] = (total / scale).T


def swap(x, axis, first):
    count = lax.axis_size(axis)
    pairs = [(i, i + 1) for i in range(first, count - 1, 2)]
    return lax.ppermute(x, axis, pairs + [(b, a) for a, b in pairs])


def shards(depth, back, graz, quality, valid, row, col, zone, tile, tide):
    down, across = lax.axis_size("ty"), lax.axis_size("tx")
    slots = down * across * RANKS
    pings = depth.shape[0]
    shape = jax.ShapeDtypeStruct
    hbm = pl.BlockSpec(memory_space=pltpu.HBM)
    block = (pings, BEAMS)
    packed = pl.pallas_call(
        pack_kernel,
        out_shape=shape((slots, FIELDS, GROUPS, LANES), F32),
        in_specs=[hbm] * 10,
        out_specs=vmem(),
        scratch_shapes=[
            pltpu.SMEM((pings,), jnp.int32),
            pltpu.SMEM((pings,), jnp.int32),
            pltpu.SMEM(tide.shape, F32),
        ]
        + [pltpu.VMEM(block, F32)] * 4
        + [pltpu.VMEM(block, jnp.int32)] * 3
        + [pltpu.SMEM((down * across,), jnp.int32), pltpu.SemaphoreType.DMA((10,))],
        compiler_params=pltpu.CompilerParams(vmem_limit_bytes=60 * 2**20),
        name="pack",
    )(tile, zone, tide, depth, back, graz, quality, valid, row, col)
    groups = [
        [(2 * chip + core) * across + i for chip in range(down // 2) for i in range(across)]
        for core in range(2)
    ]
    arrived = lax.all_to_all(
        packed, ("ty", "tx"), split_axis=0, concat_axis=0, tiled=True, axis_index_groups=groups
    )
    window = shape((CHANNELS, TILE + 8, TILE), F32)
    rim = shape((CHANNELS, 8, TILE), F32)
    ext = pltpu.VMEM((CHANNELS, TILE + 16, TILE), F32)
    mine, mates = pl.pallas_call(
        deposit_kernel,
        out_shape=(window, window),
        in_specs=[vmem()],
        out_specs=(vmem(),) * 2,
        scratch_shapes=[
            pltpu.VMEM((2, 2, 256, LANES), F32),
            pltpu.VMEM((CHANNELS, 2 * TILE, LANES), F32),
            pltpu.VMEM((slots, LANES), F32),
            pltpu.VMEM((8, slots), jnp.int32),
            pltpu.SMEM((8, slots), jnp.int32),
            pltpu.SMEM((slots // 2 + BATCH,), jnp.int32),
            pltpu.SMEM((slots // 2 + BATCH,), jnp.int32),
            pltpu.SemaphoreType.DMA,
        ],
        compiler_params=VMEM,
        name="deposit",
    )(arrived)
    total, edge = pl.pallas_call(
        join_kernel,
        out_shape=(window, rim),
        in_specs=[vmem()] * 2,
        out_specs=(vmem(),) * 2,
        compiler_params=VMEM,
        name="join",
    )(mine, swap(mates, "ty", 0))
    rows, near, far = pl.pallas_call(
        rows_kernel,
        out_shape=(shape((CHANNELS, TILE, TILE), F32), rim, rim),
        in_specs=[vmem()] * 2,
        out_specs=(vmem(),) * 3,
        scratch_shapes=[ext],
        compiler_params=VMEM,
        name="rows",
    )(total, swap(edge, "ty", 1))
    return pl.pallas_call(
        columns_kernel,
        out_shape=shape((CHANNELS, TILE, TILE), F32),
        in_specs=[vmem()] * 3,
        out_specs=vmem(),
        scratch_shapes=[ext],
        compiler_params=VMEM,
        name="columns",
    )(rows, swap(near, "tx", 0), swap(far, "tx", 1))


def solution(mesh):
    pings = P(("ty", "tx"))
    return jax.shard_map(
        shards,
        mesh=mesh,
        in_specs=(pings,) * 9 + (P(),),
        out_specs=P(None, "ty", "tx"),
        check_vma=False,
    )
```

```python
import functools
import math

import jax
import jax.numpy as jnp
from jax import lax
from jax.experimental import pallas as pl
from jax.experimental.pallas import tpu as pltpu
from jax.sharding import PartitionSpec as P

F32 = jnp.float32
BF16 = jnp.bfloat16
BEAMS = 512
CHANNELS = 8
MARGIN = 7
TILE = 64
FIELDS = 5
LANES = 128
GROUPS = BEAMS // LANES
RANKS = 2
BATCH = 32
SIGMA = 2.5
VMEM = pltpu.CompilerParams(vmem_limit_bytes=40 * 2**20)

_profile = [math.exp(-j * j / (2 * SIGMA * SIGMA)) for j in range(-MARGIN, MARGIN + 1)]
TAPS = [value / sum(_profile) for value in _profile]


def vmem():
    return pl.BlockSpec(memory_space=pltpu.VMEM)


def pack_kernel(tile_h, zone_h, tide_h, depth_h, back_h, graz_h, quality_h, valid_h, row_h, col_h, out,
                tile, zone, tide, depth, back, graz, quality, valid, row, col, cell, ready, blank, seen,
                sems, blank_sem, sent):
    pings = depth.shape[0]
    copies = [
        pltpu.make_async_copy(source, target, sems.at[i])
        for i, (source, target) in enumerate(
            (
                (tile_h, tile),
                (zone_h, zone),
                (tide_h, tide),
                (quality_h, quality),
                (valid_h, valid),
                (row_h, row),
                (col_h, col),
                (depth_h, depth),
                (back_h, back),
                (graz_h, graz),
            )
        )
    ]
    for copy in copies:
        copy.start()

    def empty(i, _):
        blank[i] = jnp.full((GROUPS, LANES), -1.0, F32)
        return 0

    lax.fori_loop(0, blank.shape[0], empty, 0, unroll=8)
    blanks = pltpu.make_async_copy(blank, out.at[:, FIELDS - 1], blank_sem)
    blanks.start()

    def clear(i, _):
        seen[i] = 0
        return 0

    lax.fori_loop(0, seen.shape[0], clear, 0, unroll=8)
    for copy in copies:
        copy.wait()
    quality[...] = quality[...] * valid[...].astype(F32)
    cell[...] = (row[...] * TILE + col[...]).astype(F32)
    blanks.wait()

    def place(p, _):
        target = tile[p]
        rank = seen[target]
        seen[target] = rank + 1
        down, across = lax.shift_right_logical(target, 4), target & 15
        chip = lax.shift_right_logical(down, 1) * 16 + across
        slot = chip * 4 + (down & 1) * 2 + rank
        offset = tide[zone[p]]
        here = pl.ds(p, 1)
        for f, field in enumerate((depth, back, graz, quality, cell)):
            values = offset - field[here, :] if f == 0 else field[here, :]
            for j in range(GROUPS):
                ready[p, f, pl.ds(j, 1), :] = values[:, j * LANES : (j + 1) * LANES]
        pltpu.make_async_copy(ready.at[p], out.at[slot], sent).start()
        return 0

    lax.fori_loop(0, pings, place, 0, unroll=4)
    pltpu.make_async_copy(ready, out.at[pl.ds(0, pings)], sent).wait()


def both(rows):
    return jnp.concatenate([rows, rows], 0).astype(BF16)


def factors(x, slot, spots):
    sub = lax.broadcasted_iota(jnp.int32, (8, LANES), 0)
    zero = jnp.zeros((16, LANES), BF16)
    one = jnp.ones((16, LANES), BF16)
    left, right = [], []
    for j in range(GROUPS):
        height, back, graz, weight, cell = (
            jnp.broadcast_to(x[slot, f, pl.ds(j, 1), :], (8, LANES)) for f in range(FIELDS)
        )
        first = jnp.where(
            (sub == 1) | (sub == 2) | (sub == 5),
            height,
            jnp.where((sub == 3) | (sub == 4), back, jnp.where(sub >= 6, graz, 1.0)),
        )
        second = jnp.where(
            sub == 2,
            height,
            jnp.where((sub == 4) | (sub == 5), back, jnp.where(sub == 7, graz, 1.0)),
        )
        stats = weight * first * second
        high = stats.astype(BF16).astype(F32)
        halves = jnp.concatenate([high, stats - high], 0).astype(BF16)
        coarse = jnp.floor(cell * (1.0 / 256.0))
        fine = both(cell - 256.0 * coarse)
        coarse = both(coarse)
        left.append(
            jnp.concatenate(
                [jnp.where(coarse == jnp.asarray(r, BF16), halves, zero) for r in range(16)], 0
            )
        )
        right.append(jnp.concatenate([jnp.where(fine == s, one, zero) for s in spots], 0))
    return jnp.concatenate(left, 1), jnp.concatenate(right, 1)


def deposit_kernel(x, mine, mates, acc, part, heads, flags_v, flags, order, sem):
    slots = x.shape[0]
    room = slots // 2 + BATCH
    core = lax.axis_index("ty") % 2

    def head(s, _):
        heads[pl.ds(s, 1), :] = x[s, FIELDS - 1, pl.ds(0, 1), :]
        return 0

    lax.fori_loop(0, slots, head, 0, unroll=16)
    pick = jnp.where(lax.broadcasted_iota(jnp.int32, (8, LANES), 1) == 0, 1.0, 0.0)
    filled = jnp.where(heads[...] >= 0.0, 1.0, 0.0)
    flags_v[...] = lax.dot_general(
        pick.astype(BF16), filled.astype(BF16), (((1,), (1,)), ((), ())),
        preferred_element_type=F32,
    ).astype(jnp.int32)
    copy = pltpu.make_async_copy(flags_v, flags, sem)
    copy.start()
    acc[...] = jnp.zeros_like(acc)
    copy.wait()

    def note(q, carry):
        counts = list(carry[:2])
        gaps = list(carry[2:])
        for side in range(2):
            for rank in range(RANKS):
                s = q * 4 + side * 2 + rank
                full = flags[0, s]
                order[side * room + counts[side]] = s
                counts[side] = counts[side] + full
                gaps[side] = jnp.where(full > 0, gaps[side], s)
        return (*counts, *gaps)

    zero = jnp.int32(0)
    found = lax.fori_loop(0, slots // 4, note, (zero, zero, zero, zero), unroll=4)
    counts, gaps = found[:2], found[2:]
    base = lax.broadcasted_iota(jnp.int32, (16, LANES), 0)
    spots = [(base + 16 * i).astype(F32).astype(BF16) for i in range(16)]
    for side in range(2):
        for u in range(BATCH):
            order[side * room + counts[side] + u] = gaps[side]

    def add(first, side, size):
        pairs = [factors(x, order[first + u], spots) for u in range(size)]
        left = jnp.concatenate([a for a, _ in pairs], 1)
        right = jnp.concatenate([b for _, b in pairs], 1)
        total = lax.dot_general(
            left, right, (((1,), (1,)), ((), ())), preferred_element_type=F32
        )
        acc[side, 0] += total[:, :LANES]
        acc[side, 1] += total[:, LANES:]

    half = BATCH // 2
    whole = [(count + half - 1) // BATCH for count in counts]
    rest = [
        jnp.minimum(jnp.maximum(count - BATCH * n, 0), 1) for count, n in zip(counts, whole)
    ]

    def step(t, _):
        side = (t >= whole[0]).astype(jnp.int32)
        add(side * room + (t - side * whole[0]) * BATCH, side, BATCH)
        return 0

    def tail(t, _):
        side = (t >= rest[0]).astype(jnp.int32)
        add(side * room + jnp.where(side > 0, whole[1], whole[0]) * BATCH, side, half)
        return 0

    lax.fori_loop(0, whole[0] + whole[1], step, 0)
    lax.fori_loop(0, rest[0] + rest[1], tail, 0)
    for side in range(2):
        for ch in range(CHANNELS):
            for piece in range(2):
                rows = acc[side, piece, pl.ds(ch, 16, stride=16), :]
                rows += acc[side, piece, pl.ds(ch + 8, 16, stride=16), :]
                for q in range(2):
                    part[ch, pl.ds(TILE * side + 2 * piece + q, 16, stride=4), 0:TILE] = rows[
                        :, q * TILE : (q + 1) * TILE
                    ]
    own = pl.ds(pl.multiple_of(core * (TILE - 8), 8), TILE + 8)
    other = pl.ds(pl.multiple_of((1 - core) * (TILE - 8), 8), TILE + 8)
    for ch in range(CHANNELS):
        mine[ch] = part[ch, own, 0:TILE]
        mates[ch] = part[ch, other, 0:TILE]


def join_kernel(mine, mates, total, rim):
    core = lax.axis_index("ty") % 2
    for ch in range(CHANNELS):
        total[ch] = mine[ch] + mates[ch]
        rim[ch] = total[ch, pl.ds(pl.multiple_of(core * TILE, 8), 8), :]


def smoothed(ext, ch):
    total = None
    for j in range(2 * MARGIN + 1):
        term = TAPS[j] * ext[ch, pl.ds(1 + j, TILE), :]
        total = term if total is None else total + term
    return total


def rows_kernel(window, rim, out, near, far, ext):
    place = lax.axis_index("ty")
    core = place % 2
    beyond = (place == 0) | (place == lax.axis_size("ty") - 1)
    odd = lax.axis_index("tx") % 2
    inside = pl.ds(pl.multiple_of(8 - core * 8, 8), TILE + 8)
    outside = pl.ds(pl.multiple_of(core * (TILE + 8), 8), 8)
    for ch in range(CHANNELS):
        ext[ch, inside, :] = window[ch]
        ext[ch, outside, :] = jnp.where(beyond, 0.0, rim[ch])
    for ch in range(CHANNELS):
        out[ch] = smoothed(ext, ch).T
        near[ch] = out[ch, pl.ds(pl.multiple_of((1 - odd) * (TILE - 8), 8), 8), :]
        far[ch] = out[ch, pl.ds(pl.multiple_of(odd * (TILE - 8), 8), 8), :]


def columns_kernel(own, near, far, out, ext):
    place = lax.axis_index("tx")
    odd = place % 2
    beyond = (place == 0) | (place == lax.axis_size("tx") - 1)
    near_rows = pl.ds(pl.multiple_of((1 - odd) * (TILE + 8), 8), 8)
    far_rows = pl.ds(pl.multiple_of(odd * (TILE + 8), 8), 8)
    for ch in range(CHANNELS):
        ext[ch, 8 : 8 + TILE, :] = own[ch]
        ext[ch, near_rows, :] = near[ch]
        ext[ch, far_rows, :] = jnp.where(beyond, 0.0, far[ch])
    scale = None
    for ch in range(CHANNELS):
        total = smoothed(ext, ch)
        if ch == 0:
            scale = 1.0 + total
        out[ch] = (total / scale).T


def swap(x, axis, first):
    count = lax.axis_size(axis)
    pairs = [(i, (i + 1) % count) for i in range(first, count, 2)]
    return lax.ppermute(x, axis, pairs + [(b, a) for a, b in pairs])


def shards(depth, back, graz, quality, valid, row, col, zone, tile, tide):
    down, across = lax.axis_size("ty"), lax.axis_size("tx")
    slots = down * across * RANKS
    pings = depth.shape[0]
    shape = jax.ShapeDtypeStruct
    hbm = pl.BlockSpec(memory_space=pltpu.HBM)
    block = (pings, BEAMS)
    packed = pl.pallas_call(
        pack_kernel,
        out_shape=shape((slots, FIELDS, GROUPS, LANES), F32),
        in_specs=[hbm] * 10,
        out_specs=hbm,
        scratch_shapes=[
            pltpu.SMEM((pings,), jnp.int32),
            pltpu.SMEM((pings,), jnp.int32),
            pltpu.SMEM(tide.shape, F32),
        ]
        + [pltpu.VMEM(block, F32)] * 4
        + [pltpu.VMEM(block, jnp.int32)] * 3
        + [
            pltpu.VMEM(block, F32),
            pltpu.VMEM((pings, FIELDS, GROUPS, LANES), F32),
            pltpu.VMEM((slots, GROUPS, LANES), F32),
            pltpu.SMEM((down * across,), jnp.int32),
            pltpu.SemaphoreType.DMA((10,)),
            pltpu.SemaphoreType.DMA,
            pltpu.SemaphoreType.DMA,
        ],
        compiler_params=pltpu.CompilerParams(vmem_limit_bytes=60 * 2**20),
        name="pack",
    )(tile, zone, tide, depth, back, graz, quality, valid, row, col)
    groups = [
        [(2 * chip + core) * across + i for chip in range(down // 2) for i in range(across)]
        for core in range(2)
    ]
    arrived = lax.all_to_all(
        packed, ("ty", "tx"), split_axis=0, concat_axis=0, tiled=True, axis_index_groups=groups
    )
    window = shape((CHANNELS, TILE + 8, TILE), F32)
    rim = shape((CHANNELS, 8, TILE), F32)
    ext = pltpu.VMEM((CHANNELS, TILE + 16, TILE), F32)
    mine, mates = pl.pallas_call(
        deposit_kernel,
        out_shape=(window, window),
        in_specs=[vmem()],
        out_specs=(vmem(),) * 2,
        scratch_shapes=[
            pltpu.VMEM((2, 2, 256, LANES), F32),
            pltpu.VMEM((CHANNELS, 2 * TILE, LANES), F32),
            pltpu.VMEM((slots, LANES), F32),
            pltpu.VMEM((8, slots), jnp.int32),
            pltpu.SMEM((8, slots), jnp.int32),
            pltpu.SMEM((slots + 2 * BATCH,), jnp.int32),
            pltpu.SemaphoreType.DMA,
        ],
        compiler_params=VMEM,
        name="deposit",
    )(arrived)
    total, edge = pl.pallas_call(
        join_kernel,
        out_shape=(window, rim),
        in_specs=[vmem()] * 2,
        out_specs=(vmem(),) * 2,
        compiler_params=VMEM,
        name="join",
    )(mine, swap(mates, "ty", 0))
    rows, near, far = pl.pallas_call(
        rows_kernel,
        out_shape=(shape((CHANNELS, TILE, TILE), F32), rim, rim),
        in_specs=[vmem()] * 2,
        out_specs=(vmem(),) * 3,
        scratch_shapes=[ext],
        compiler_params=VMEM,
        name="rows",
    )(total, swap(edge, "ty", 1))
    return pl.pallas_call(
        columns_kernel,
        out_shape=shape((CHANNELS, TILE, TILE), F32),
        in_specs=[vmem()] * 3,
        out_specs=vmem(),
        scratch_shapes=[ext],
        compiler_params=VMEM,
        name="columns",
    )(rows, swap(near, "tx", 0), swap(far, "tx", 1))


def solution(mesh):
    pings = P(("ty", "tx"))
    return jax.shard_map(
        shards,
        mesh=mesh,
        in_specs=(pings,) * 9 + (P(),),
        out_specs=P(None, "ty", "tx"),
        check_vma=False,
    )
```

```python
import functools
import math

import jax
import jax.numpy as jnp
from jax import lax
from jax.experimental import pallas as pl
from jax.experimental.pallas import tpu as pltpu
from jax.sharding import PartitionSpec as P

F32 = jnp.float32
BF16 = jnp.bfloat16
BEAMS = 512
CHANNELS = 8
MARGIN = 7
TILE = 64
FIELDS = 5
LANES = 128
GROUPS = BEAMS // LANES
RANKS = 2
BATCH = 32
SIGMA = 2.5
VMEM = pltpu.CompilerParams(vmem_limit_bytes=40 * 2**20)

_profile = [math.exp(-j * j / (2 * SIGMA * SIGMA)) for j in range(-MARGIN, MARGIN + 1)]
TAPS = [value / sum(_profile) for value in _profile]


def vmem():
    return pl.BlockSpec(memory_space=pltpu.VMEM)


def pack_kernel(tile_h, zone_h, tide_h, depth_h, back_h, graz_h, quality_h, valid_h, row_h, col_h, out,
                tile, zone, tide, depth, back, graz, quality, valid, row, col, cell, ready, blank, seen,
                sems, blank_sem, sent):
    pings = depth.shape[0]
    copies = [
        pltpu.make_async_copy(source, target, sems.at[i])
        for i, (source, target) in enumerate(
            (
                (tile_h, tile),
                (zone_h, zone),
                (tide_h, tide),
                (quality_h, quality),
                (valid_h, valid),
                (row_h, row),
                (col_h, col),
                (depth_h, depth),
                (back_h, back),
                (graz_h, graz),
            )
        )
    ]
    for copy in copies:
        copy.start()

    def empty(i, _):
        blank[i] = jnp.full((GROUPS, LANES), -1.0, F32)
        return 0

    lax.fori_loop(0, blank.shape[0], empty, 0, unroll=8)
    blanks = pltpu.make_async_copy(blank, out.at[:, FIELDS - 1], blank_sem)
    blanks.start()

    def clear(i, _):
        seen[i] = 0
        return 0

    lax.fori_loop(0, seen.shape[0], clear, 0, unroll=8)
    for copy in copies:
        copy.wait()
    quality[...] = quality[...] * valid[...].astype(F32)
    cell[...] = (row[...] * TILE + col[...]).astype(F32)
    blanks.wait()

    def place(p, _):
        target = tile[p]
        rank = seen[target]
        seen[target] = rank + 1
        down, across = lax.shift_right_logical(target, 4), target & 15
        chip = lax.shift_right_logical(down, 1) * 16 + across
        slot = chip * 4 + (down & 1) * 2 + rank
        offset = tide[zone[p]]
        here = pl.ds(p, 1)
        for f, field in enumerate((depth, back, graz, quality, cell)):
            values = offset - field[here, :] if f == 0 else field[here, :]
            for j in range(GROUPS):
                ready[p, f, pl.ds(j, 1), :] = values[:, j * LANES : (j + 1) * LANES]
        pltpu.make_async_copy(ready.at[p], out.at[slot], sent).start()
        return 0

    lax.fori_loop(0, pings, place, 0, unroll=4)
    pltpu.make_async_copy(ready, out.at[pl.ds(0, pings)], sent).wait()


def both(rows):
    return jnp.concatenate([rows, rows], 0).astype(BF16)


def factors(x, slot, spots):
    sub = lax.broadcasted_iota(jnp.int32, (8, LANES), 0)
    zero = jnp.zeros((16, LANES), BF16)
    one = jnp.ones((16, LANES), BF16)
    left, right = [], []
    for j in range(GROUPS):
        height, back, graz, weight, cell = (
            jnp.broadcast_to(x[slot, f, pl.ds(j, 1), :], (8, LANES)) for f in range(FIELDS)
        )
        first = jnp.where(
            (sub == 1) | (sub == 2) | (sub == 5),
            height,
            jnp.where((sub == 3) | (sub == 4), back, jnp.where(sub >= 6, graz, 1.0)),
        )
        second = jnp.where(
            sub == 2,
            height,
            jnp.where((sub == 4) | (sub == 5), back, jnp.where(sub == 7, graz, 1.0)),
        )
        stats = weight * first * second
        high = stats.astype(BF16).astype(F32)
        halves = jnp.concatenate([high, stats - high], 0).astype(BF16)
        coarse = jnp.floor(cell * (1.0 / 256.0))
        fine = both(cell - 256.0 * coarse)
        coarse = both(coarse)
        left.append(
            jnp.concatenate(
                [jnp.where(coarse == jnp.asarray(r, BF16), halves, zero) for r in range(16)], 0
            )
        )
        right.append(jnp.concatenate([jnp.where(fine == s, one, zero) for s in spots], 0))
    return jnp.concatenate(left, 1), jnp.concatenate(right, 1)


def deposit_kernel(x, mine, mates, acc, part, heads, flags_v, flags, order, sem):
    slots = x.shape[0]
    room = slots // 2 + BATCH
    core = lax.axis_index("ty") % 2

    def head(s, _):
        heads[pl.ds(s, 1), :] = x[s, FIELDS - 1, pl.ds(0, 1), :]
        return 0

    lax.fori_loop(0, slots, head, 0, unroll=16)
    pick = jnp.where(lax.broadcasted_iota(jnp.int32, (8, LANES), 1) == 0, 1.0, 0.0)
    filled = jnp.where(heads[...] >= 0.0, 1.0, 0.0)
    flags_v[...] = lax.dot_general(
        pick.astype(BF16), filled.astype(BF16), (((1,), (1,)), ((), ())),
        preferred_element_type=F32,
    ).astype(jnp.int32)
    copy = pltpu.make_async_copy(flags_v, flags, sem)
    copy.start()
    acc[...] = jnp.zeros_like(acc)
    copy.wait()

    def note(q, carry):
        counts = list(carry[:2])
        gaps = list(carry[2:])
        for side in range(2):
            for rank in range(RANKS):
                s = q * 4 + side * 2 + rank
                full = flags[0, s]
                order[side * room + counts[side]] = s
                counts[side] = counts[side] + full
                gaps[side] = jnp.where(full > 0, gaps[side], s)
        return (*counts, *gaps)

    zero = jnp.int32(0)
    found = lax.fori_loop(0, slots // 4, note, (zero, zero, zero, zero), unroll=4)
    counts, gaps = found[:2], found[2:]
    base = lax.broadcasted_iota(jnp.int32, (16, LANES), 0)
    spots = [(base + 16 * i).astype(F32).astype(BF16) for i in range(16)]
    for side in range(2):
        for u in range(BATCH):
            order[side * room + counts[side] + u] = gaps[side]

    def add(first, side, size):
        pairs = [factors(x, order[first + u], spots) for u in range(size)]
        left = jnp.concatenate([a for a, _ in pairs], 1)
        right = jnp.concatenate([b for _, b in pairs], 1)
        total = lax.dot_general(
            left, right, (((1,), (1,)), ((), ())), preferred_element_type=F32
        )
        acc[side, 0] += total[:, :LANES]
        acc[side, 1] += total[:, LANES:]

    half = BATCH // 2
    whole = [(count + half - 1) // BATCH for count in counts]
    rest = [
        jnp.minimum(jnp.maximum(count - BATCH * n, 0), 1) for count, n in zip(counts, whole)
    ]

    def step(t, _):
        side = (t >= whole[0]).astype(jnp.int32)
        add(side * room + (t - side * whole[0]) * BATCH, side, BATCH)
        return 0

    def tail(t, _):
        side = (t >= rest[0]).astype(jnp.int32)
        add(side * room + jnp.where(side > 0, whole[1], whole[0]) * BATCH, side, half)
        return 0

    lax.fori_loop(0, whole[0] + whole[1], step, 0)
    lax.fori_loop(0, rest[0] + rest[1], tail, 0)
    for side in range(2):
        for ch in range(CHANNELS):
            for piece in range(2):
                rows = acc[side, piece, pl.ds(ch, 16, stride=16), :]
                rows += acc[side, piece, pl.ds(ch + 8, 16, stride=16), :]
                for q in range(2):
                    part[ch, pl.ds(TILE * side + 2 * piece + q, 16, stride=4), 0:TILE] = rows[
                        :, q * TILE : (q + 1) * TILE
                    ]
    own = pl.ds(pl.multiple_of(core * (TILE - 8), 8), TILE + 8)
    other = pl.ds(pl.multiple_of((1 - core) * (TILE - 8), 8), TILE + 8)
    for ch in range(CHANNELS):
        mine[ch] = part[ch, own, 0:TILE]
        mates[ch] = part[ch, other, 0:TILE]


def join_kernel(mine, mates, total, rim, near, far, near_corner, far_corner):
    core = lax.axis_index("ty") % 2
    odd = lax.axis_index("tx") % 2
    outer = pl.ds(pl.multiple_of(core * TILE, 8), 8)
    first, last = [], []
    for ch in range(CHANNELS):
        both_cores = mine[ch] + mates[ch]
        total[ch] = both_cores
        rim[ch] = total[ch, outer, :]
        first.append(both_cores[:, 0:8])
        last.append(both_cores[:, TILE - 8 : TILE])
    first, last = jnp.concatenate(first, 1), jnp.concatenate(last, 1)
    near[...] = jnp.where(odd == 1, first, last)
    far[...] = jnp.where(odd == 1, last, first)
    near_corner[...] = near[outer, :]
    far_corner[...] = far[outer, :]


def smoothed(ext):
    total = None
    for j in range(2 * MARGIN + 1):
        term = TAPS[j] * ext[pl.ds(1 + j, TILE), :]
        total = term if total is None else total + term
    return total


def smooth_kernel(window, rim, near, far, near_corner, far_corner, out, ext, side, turned):
    down, across = lax.axis_index("ty"), lax.axis_index("tx")
    core, odd = down % 2, across % 2
    no_row = (down == 0) | (down == lax.axis_size("ty") - 1)
    no_column = (across == 0) | (across == lax.axis_size("tx") - 1)
    inside = pl.ds(pl.multiple_of(8 - core * 8, 8), TILE + 8)
    outside = pl.ds(pl.multiple_of(core * (TILE + 8), 8), 8)
    for ch in range(CHANNELS):
        ext[ch, inside, :] = window[ch]
        ext[ch, outside, :] = jnp.where(no_row, 0.0, rim[ch])
        turned[ch, 8 : 8 + TILE, :] = smoothed(ext.at[ch]).T
    for strip, corner, missing, start in (
        (near, near_corner, False, 1 - odd),
        (far, far_corner, no_column, odd),
    ):
        side[inside, :] = strip[...] if missing is False else jnp.where(missing, 0.0, strip[...])
        gone = no_row if missing is False else no_row | missing
        side[outside, :] = jnp.where(gone, 0.0, corner[...])
        columns = smoothed(side).T
        place = pl.ds(pl.multiple_of(start * (TILE + 8), 8), 8)
        for ch in range(CHANNELS):
            turned[ch, place, :] = columns[ch * 8 : ch * 8 + 8]
    scale = None
    for ch in range(CHANNELS):
        total = smoothed(turned.at[ch])
        if ch == 0:
            scale = 1.0 + total
        out[ch] = (total / scale).T


def partner(place, first, count):
    step = 1 if (place - first) % 2 == 0 else -1
    return (place + step) % count


def swap(x, down, across):
    rows, columns = lax.axis_size("ty"), lax.axis_size("tx")
    return lax.ppermute(
        x,
        ("ty", "tx"),
        [
            (i * columns + j, down(i) * columns + across(j))
            for i in range(rows)
            for j in range(columns)
        ],
    )


def shards(depth, back, graz, quality, valid, row, col, zone, tile, tide):
    down, across = lax.axis_size("ty"), lax.axis_size("tx")
    slots = down * across * RANKS
    pings = depth.shape[0]
    shape = jax.ShapeDtypeStruct
    hbm = pl.BlockSpec(memory_space=pltpu.HBM)
    block = (pings, BEAMS)
    packed = pl.pallas_call(
        pack_kernel,
        out_shape=shape((slots, FIELDS, GROUPS, LANES), F32),
        in_specs=[hbm] * 10,
        out_specs=hbm,
        scratch_shapes=[
            pltpu.SMEM((pings,), jnp.int32),
            pltpu.SMEM((pings,), jnp.int32),
            pltpu.SMEM(tide.shape, F32),
        ]
        + [pltpu.VMEM(block, F32)] * 4
        + [pltpu.VMEM(block, jnp.int32)] * 3
        + [
            pltpu.VMEM(block, F32),
            pltpu.VMEM((pings, FIELDS, GROUPS, LANES), F32),
            pltpu.VMEM((slots, GROUPS, LANES), F32),
            pltpu.SMEM((down * across,), jnp.int32),
            pltpu.SemaphoreType.DMA((10,)),
            pltpu.SemaphoreType.DMA,
            pltpu.SemaphoreType.DMA,
        ],
        compiler_params=pltpu.CompilerParams(vmem_limit_bytes=60 * 2**20),
        name="pack",
    )(tile, zone, tide, depth, back, graz, quality, valid, row, col)
    groups = [
        [(2 * chip + core) * across + i for chip in range(down // 2) for i in range(across)]
        for core in range(2)
    ]
    arrived = lax.all_to_all(
        packed, ("ty", "tx"), split_axis=0, concat_axis=0, tiled=True, axis_index_groups=groups
    )
    window = shape((CHANNELS, TILE + 8, TILE), F32)
    mine, mates = pl.pallas_call(
        deposit_kernel,
        out_shape=(window, window),
        in_specs=[vmem()],
        out_specs=(vmem(),) * 2,
        scratch_shapes=[
            pltpu.VMEM((2, 2, 256, LANES), F32),
            pltpu.VMEM((CHANNELS, 2 * TILE, LANES), F32),
            pltpu.VMEM((slots, LANES), F32),
            pltpu.VMEM((8, slots), jnp.int32),
            pltpu.SMEM((8, slots), jnp.int32),
            pltpu.SMEM((slots + 2 * BATCH,), jnp.int32),
            pltpu.SemaphoreType.DMA,
        ],
        compiler_params=VMEM,
        name="deposit",
    )(arrived)
    same = lambda i: i
    mate = functools.partial(partner, first=0, count=down)
    next_chip = functools.partial(partner, first=1, count=down)
    near_by = functools.partial(partner, first=0, count=across)
    far_off = functools.partial(partner, first=1, count=across)
    strip = shape((TILE + 8, CHANNELS * 8), F32)
    corner = shape((8, CHANNELS * 8), F32)
    total, rim, near, far, near_corner, far_corner = pl.pallas_call(
        join_kernel,
        out_shape=(window, shape((CHANNELS, 8, TILE), F32), strip, strip, corner, corner),
        in_specs=[vmem()] * 2,
        out_specs=(vmem(),) * 6,
        compiler_params=VMEM,
        name="join",
    )(mine, swap(mates, mate, same))
    ext = pltpu.VMEM((CHANNELS, TILE + 16, TILE), F32)
    return pl.pallas_call(
        smooth_kernel,
        out_shape=shape((CHANNELS, TILE, TILE), F32),
        in_specs=[vmem()] * 6,
        out_specs=vmem(),
        scratch_shapes=[ext, pltpu.VMEM((TILE + 16, CHANNELS * 8), F32), ext],
        compiler_params=VMEM,
        name="smooth",
    )(
        total,
        swap(rim, next_chip, same),
        swap(near, same, near_by),
        swap(far, same, far_off),
        swap(near_corner, next_chip, near_by),
        swap(far_corner, next_chip, far_off),
    )


def solution(mesh):
    pings = P(("ty", "tx"))
    return jax.shard_map(
        shards,
        mesh=mesh,
        in_specs=(pings,) * 9 + (P(),),
        out_specs=P(None, "ty", "tx"),
        check_vma=False,
    )
```

```python
import functools
import math

import jax
import jax.numpy as jnp
from jax import lax
from jax.experimental import pallas as pl
from jax.experimental.pallas import tpu as pltpu
from jax.sharding import PartitionSpec as P

F32 = jnp.float32
BF16 = jnp.bfloat16
BEAMS = 512
CHANNELS = 8
MARGIN = 7
TILE = 64
FIELDS = 5
LANES = 128
GROUPS = BEAMS // LANES
RANKS = 2
BATCH = 32
TAIL = 8
SIGMA = 2.5
VMEM = pltpu.CompilerParams(vmem_limit_bytes=40 * 2**20)

_profile = [math.exp(-j * j / (2 * SIGMA * SIGMA)) for j in range(-MARGIN, MARGIN + 1)]
TAPS = [value / sum(_profile) for value in _profile]


def vmem():
    return pl.BlockSpec(memory_space=pltpu.VMEM)


def pack_kernel(tile_h, zone_h, tide_h, depth_h, back_h, graz_h, quality_h, valid_h, row_h, col_h, out,
                tile, zone, tide, depth, back, graz, quality, valid, row, col, cell, ready, blank, seen,
                sems, blank_sem, sent):
    pings = depth.shape[0]
    copies = [
        pltpu.make_async_copy(source, target, sems.at[i])
        for i, (source, target) in enumerate(
            (
                (tile_h, tile),
                (zone_h, zone),
                (tide_h, tide),
                (quality_h, quality),
                (valid_h, valid),
                (row_h, row),
                (col_h, col),
                (depth_h, depth),
                (back_h, back),
                (graz_h, graz),
            )
        )
    ]
    for copy in copies:
        copy.start()

    def empty(i, _):
        blank[i] = jnp.full((GROUPS, LANES), -1.0, F32)
        return 0

    lax.fori_loop(0, blank.shape[0], empty, 0, unroll=8)
    blanks = pltpu.make_async_copy(blank, out.at[:, FIELDS - 1], blank_sem)
    blanks.start()

    def clear(i, _):
        seen[i] = 0
        return 0

    lax.fori_loop(0, seen.shape[0], clear, 0, unroll=8)
    for copy in copies:
        copy.wait()
    quality[...] = quality[...] * valid[...].astype(F32)
    cell[...] = (row[...] * TILE + col[...]).astype(F32)
    blanks.wait()

    def place(p, _):
        target = tile[p]
        rank = seen[target]
        seen[target] = rank + 1
        down, across = lax.shift_right_logical(target, 4), target & 15
        chip = lax.shift_right_logical(down, 1) * 16 + across
        slot = chip * 4 + (down & 1) * 2 + rank
        offset = tide[zone[p]]
        here = pl.ds(p, 1)
        for f, field in enumerate((depth, back, graz, quality, cell)):
            values = offset - field[here, :] if f == 0 else field[here, :]
            for j in range(GROUPS):
                ready[p, f, pl.ds(j, 1), :] = values[:, j * LANES : (j + 1) * LANES]
        pltpu.make_async_copy(ready.at[p], out.at[slot], sent).start()
        return 0

    lax.fori_loop(0, pings, place, 0, unroll=8)
    pltpu.make_async_copy(ready, out.at[pl.ds(0, pings)], sent).wait()


def both(rows):
    return jnp.concatenate([rows, rows], 0).astype(BF16)


def factors(x, slot, spots):
    sub = lax.broadcasted_iota(jnp.int32, (8, LANES), 0)
    zero = jnp.zeros((16, LANES), BF16)
    one = jnp.ones((16, LANES), BF16)
    left, right = [], []
    for j in range(GROUPS):
        height, back, graz, weight, cell = (
            jnp.broadcast_to(x[slot, f, pl.ds(j, 1), :], (8, LANES)) for f in range(FIELDS)
        )
        first = jnp.where(
            (sub == 1) | (sub == 2) | (sub == 5),
            height,
            jnp.where((sub == 3) | (sub == 4), back, jnp.where(sub >= 6, graz, 1.0)),
        )
        second = jnp.where(
            sub == 2,
            height,
            jnp.where((sub == 4) | (sub == 5), back, jnp.where(sub == 7, graz, 1.0)),
        )
        stats = weight * first * second
        high = stats.astype(BF16).astype(F32)
        halves = jnp.concatenate([high, stats - high], 0).astype(BF16)
        coarse = jnp.floor(cell * (1.0 / 256.0))
        fine = both(cell - 256.0 * coarse)
        coarse = both(coarse)
        left.append(
            jnp.concatenate(
                [jnp.where(coarse == jnp.asarray(r, BF16), halves, zero) for r in range(16)], 0
            )
        )
        right.append(jnp.concatenate([jnp.where(fine == s, one, zero) for s in spots], 0))
    return jnp.concatenate(left, 1), jnp.concatenate(right, 1)


def deposit_kernel(x, mine, mates, acc, part, heads, table_v, table, sem):
    slots = x.shape[0]
    core = lax.axis_index("ty") % 2

    def head(s, _):
        heads[pl.ds(s, 1), :] = x[s, FIELDS - 1, pl.ds(0, 1), :]
        return 0

    lax.fori_loop(0, slots, head, 0, unroll=16)
    lane = lax.broadcasted_iota(jnp.int32, (8, slots), 1)
    pick = jnp.where(lax.broadcasted_iota(jnp.int32, (8, LANES), 1) == 0, 1.0, 0.0)
    filled = jnp.where(heads[...] >= 0.0, 1.0, 0.0)
    full = lax.dot_general(
        pick.astype(BF16), filled.astype(BF16), (((1,), (1,)), ((), ())),
        preferred_element_type=F32,
    )
    i = lax.broadcasted_iota(jnp.int32, (slots, slots), 0)
    j = lax.broadcasted_iota(jnp.int32, (slots, slots), 1)
    before = jnp.where((i < j) & ((i & 2) == (j & 2)), 1.0, 0.0).astype(BF16)
    position = jnp.dot(full.astype(BF16), before, preferred_element_type=F32)
    numbers = jnp.concatenate([lane.astype(F32), jnp.ones((8, slots), F32)], 0).astype(BF16)
    wanted = i.astype(F32)
    for side in range(2):
        ours = (lane & 2) == 2 * side
        key = jnp.where(ours & (full > 0.0), position, -1.0)
        match = jnp.where(jnp.broadcast_to(key[0:1], (slots, slots)) == wanted, 1.0, 0.0)
        found = lax.dot_general(
            numbers, match.astype(BF16), (((1,), (1,)), ((), ())), preferred_element_type=F32
        )
        gap = jnp.max(
            jnp.where(ours & (full == 0.0), lane.astype(F32), -1.0), axis=1, keepdims=True
        )
        count = jnp.sum(found[8:], axis=1, keepdims=True)
        listed = found[:8] + (1.0 - found[8:]) * gap
        table_v[side] = jnp.where(lane == slots - 1, count, listed).astype(jnp.int32)
    copy = pltpu.make_async_copy(table_v, table, sem)
    copy.start()
    acc[...] = jnp.zeros_like(acc)
    base = lax.broadcasted_iota(jnp.int32, (16, LANES), 0)
    spots = [(base + 16 * k).astype(F32).astype(BF16) for k in range(16)]
    copy.wait()
    counts = [table[side, 0, slots - 1] for side in range(2)]

    def add(first, side, size):
        pairs = [factors(x, table[side, 0, first + u], spots) for u in range(size)]
        left = jnp.concatenate([a for a, _ in pairs], 1)
        right = jnp.concatenate([b for _, b in pairs], 1)
        total = lax.dot_general(
            left, right, (((1,), (1,)), ((), ())), preferred_element_type=F32
        )
        acc[side, 0] += total[:, :LANES]
        acc[side, 1] += total[:, LANES:]

    whole = [(count + TAIL - 1) // BATCH for count in counts]
    rest = [
        (jnp.maximum(count - BATCH * n, 0) + TAIL - 1) // TAIL for count, n in zip(counts, whole)
    ]

    def step(t, _):
        side = (t >= whole[0]).astype(jnp.int32)
        add((t - side * whole[0]) * BATCH, side, BATCH)
        return 0

    def tail(t, _):
        side = (t >= rest[0]).astype(jnp.int32)
        start = jnp.where(side > 0, whole[1], whole[0]) * BATCH
        add(start + (t - side * rest[0]) * TAIL, side, TAIL)
        return 0

    lax.fori_loop(0, whole[0] + whole[1], step, 0)
    lax.fori_loop(0, rest[0] + rest[1], tail, 0)
    for side in range(2):
        for ch in range(CHANNELS):
            for piece in range(2):
                rows = acc[side, piece, pl.ds(ch, 16, stride=16), :]
                rows += acc[side, piece, pl.ds(ch + 8, 16, stride=16), :]
                for q in range(2):
                    part[ch, pl.ds(TILE * side + 2 * piece + q, 16, stride=4), 0:TILE] = rows[
                        :, q * TILE : (q + 1) * TILE
                    ]
    own = pl.ds(pl.multiple_of(core * (TILE - 8), 8), TILE + 8)
    other = pl.ds(pl.multiple_of((1 - core) * (TILE - 8), 8), TILE + 8)
    for ch in range(CHANNELS):
        mine[ch] = part[ch, own, 0:TILE]
        mates[ch] = part[ch, other, 0:TILE]


def join_kernel(mine, mates, total, rim):
    core = lax.axis_index("ty") % 2
    for ch in range(CHANNELS):
        total[ch] = mine[ch] + mates[ch]
        rim[ch] = total[ch, pl.ds(pl.multiple_of(core * TILE, 8), 8), :]


def smoothed(ext, ch):
    total = None
    for j in range(2 * MARGIN + 1):
        term = TAPS[j] * ext[ch, pl.ds(1 + j, TILE), :]
        total = term if total is None else total + term
    return total


def rows_kernel(window, rim, out, near, far, ext):
    place = lax.axis_index("ty")
    core = place % 2
    beyond = (place == 0) | (place == lax.axis_size("ty") - 1)
    odd = lax.axis_index("tx") % 2
    inside = pl.ds(pl.multiple_of(8 - core * 8, 8), TILE + 8)
    outside = pl.ds(pl.multiple_of(core * (TILE + 8), 8), 8)
    for ch in range(CHANNELS):
        ext[ch, inside, :] = window[ch]
        ext[ch, outside, :] = jnp.where(beyond, 0.0, rim[ch])
    for ch in range(CHANNELS):
        out[ch] = smoothed(ext, ch).T
        near[ch] = out[ch, pl.ds(pl.multiple_of((1 - odd) * (TILE - 8), 8), 8), :]
        far[ch] = out[ch, pl.ds(pl.multiple_of(odd * (TILE - 8), 8), 8), :]


def inner_kernel(own, out, ext):
    for ch in range(CHANNELS):
        ext[ch, 0:8, :] = jnp.zeros((8, TILE), F32)
        ext[ch, 8 : 8 + TILE, :] = own[ch]
        ext[ch, 8 + TILE : 16 + TILE, :] = jnp.zeros((8, TILE), F32)
    for ch in range(CHANNELS):
        out[ch] = smoothed(ext, ch)


def columns_kernel(own, inner, near, far, out, ext):
    place = lax.axis_index("tx")
    odd = place % 2
    beyond = (place == 0) | (place == lax.axis_size("tx") - 1)
    near_rows = pl.ds(pl.multiple_of((1 - odd) * 40, 8), 8)
    far_rows = pl.ds(pl.multiple_of(odd * 40, 8), 8)
    for ch in range(CHANNELS):
        ext[ch, 8:24, :] = own[ch, 0:16]
        ext[ch, 24:40, :] = own[ch, TILE - 16 : TILE]
        ext[ch, near_rows, :] = near[ch]
        ext[ch, far_rows, :] = jnp.where(beyond, 0.0, far[ch])
    scale = None
    for ch in range(CHANNELS):
        ends = []
        for first in (1, 25):
            total = None
            for j in range(2 * MARGIN + 1):
                term = TAPS[j] * ext[ch, pl.ds(first + j, 8), :]
                total = term if total is None else total + term
            ends.append(total)
        total = jnp.concatenate([ends[0], inner[ch, 8 : TILE - 8], ends[1]], 0)
        if ch == 0:
            scale = 1.0 + total
        out[ch] = (total / scale).T


def swap(x, axis, first):
    count = lax.axis_size(axis)
    pairs = [(i, (i + 1) % count) for i in range(first, count, 2)]
    return lax.ppermute(x, axis, pairs + [(b, a) for a, b in pairs])


def shards(depth, back, graz, quality, valid, row, col, zone, tile, tide):
    down, across = lax.axis_size("ty"), lax.axis_size("tx")
    slots = down * across * RANKS
    pings = depth.shape[0]
    shape = jax.ShapeDtypeStruct
    hbm = pl.BlockSpec(memory_space=pltpu.HBM)
    block = (pings, BEAMS)
    packed = pl.pallas_call(
        pack_kernel,
        out_shape=shape((slots, FIELDS, GROUPS, LANES), F32),
        in_specs=[hbm] * 10,
        out_specs=hbm,
        scratch_shapes=[
            pltpu.SMEM((pings,), jnp.int32),
            pltpu.SMEM((pings,), jnp.int32),
            pltpu.SMEM(tide.shape, F32),
        ]
        + [pltpu.VMEM(block, F32)] * 4
        + [pltpu.VMEM(block, jnp.int32)] * 3
        + [
            pltpu.VMEM(block, F32),
            pltpu.VMEM((pings, FIELDS, GROUPS, LANES), F32),
            pltpu.VMEM((slots, GROUPS, LANES), F32),
            pltpu.SMEM((down * across,), jnp.int32),
            pltpu.SemaphoreType.DMA((10,)),
            pltpu.SemaphoreType.DMA,
            pltpu.SemaphoreType.DMA,
        ],
        compiler_params=pltpu.CompilerParams(vmem_limit_bytes=60 * 2**20),
        name="pack",
    )(tile, zone, tide, depth, back, graz, quality, valid, row, col)
    groups = [
        [(2 * chip + core) * across + i for chip in range(down // 2) for i in range(across)]
        for core in range(2)
    ]
    arrived = lax.all_to_all(
        packed, ("ty", "tx"), split_axis=0, concat_axis=0, tiled=True, axis_index_groups=groups
    )
    window = shape((CHANNELS, TILE + 8, TILE), F32)
    rim = shape((CHANNELS, 8, TILE), F32)
    ext = pltpu.VMEM((CHANNELS, TILE + 16, TILE), F32)
    mine, mates = pl.pallas_call(
        deposit_kernel,
        out_shape=(window, window),
        in_specs=[vmem()],
        out_specs=(vmem(),) * 2,
        scratch_shapes=[
            pltpu.VMEM((2, 2, 256, LANES), F32),
            pltpu.VMEM((CHANNELS, 2 * TILE, LANES), F32),
            pltpu.VMEM((slots, LANES), F32),
            pltpu.VMEM((2, 8, slots), jnp.int32),
            pltpu.SMEM((2, 8, slots), jnp.int32),
            pltpu.SemaphoreType.DMA,
        ],
        compiler_params=VMEM,
        name="deposit",
    )(arrived)
    total, edge = pl.pallas_call(
        join_kernel,
        out_shape=(window, rim),
        in_specs=[vmem()] * 2,
        out_specs=(vmem(),) * 2,
        compiler_params=VMEM,
        name="join",
    )(mine, swap(mates, "ty", 0))
    rows, near, far = pl.pallas_call(
        rows_kernel,
        out_shape=(shape((CHANNELS, TILE, TILE), F32), rim, rim),
        in_specs=[vmem()] * 2,
        out_specs=(vmem(),) * 3,
        scratch_shapes=[ext],
        compiler_params=VMEM,
        name="rows",
    )(total, swap(edge, "ty", 1))
    near, far = swap(near, "tx", 0), swap(far, "tx", 1)
    inner = pl.pallas_call(
        inner_kernel,
        out_shape=shape((CHANNELS, TILE, TILE), F32),
        in_specs=[vmem()],
        out_specs=vmem(),
        scratch_shapes=[ext],
        compiler_params=VMEM,
        cost_estimate=pl.CostEstimate(flops=10**7, bytes_accessed=10**6, transcendentals=0),
        name="inner",
    )(rows)
    return pl.pallas_call(
        columns_kernel,
        out_shape=shape((CHANNELS, TILE, TILE), F32),
        in_specs=[vmem()] * 4,
        out_specs=vmem(),
        scratch_shapes=[pltpu.VMEM((CHANNELS, 48, TILE), F32)],
        compiler_params=VMEM,
        name="columns",
    )(rows, inner, near, far)


def solution(mesh):
    pings = P(("ty", "tx"))
    return jax.shard_map(
        shards,
        mesh=mesh,
        in_specs=(pings,) * 9 + (P(),),
        out_specs=P(None, "ty", "tx"),
        check_vma=False,
    )
```

```python
import functools
import math

import jax
import jax.numpy as jnp
from jax import lax
from jax.experimental import pallas as pl
from jax.experimental.pallas import tpu as pltpu
from jax.sharding import PartitionSpec as P

F32 = jnp.float32
BF16 = jnp.bfloat16
BEAMS = 512
CHANNELS = 8
MARGIN = 7
TILE = 64
FIELDS = 5
LANES = 128
GROUPS = BEAMS // LANES
RANKS = 2
BATCH = 32
TAIL = 8
SIGMA = 2.5
VMEM = pltpu.CompilerParams(vmem_limit_bytes=40 * 2**20)

_profile = [math.exp(-j * j / (2 * SIGMA * SIGMA)) for j in range(-MARGIN, MARGIN + 1)]
TAPS = [value / sum(_profile) for value in _profile]


def vmem():
    return pl.BlockSpec(memory_space=pltpu.VMEM)


def pack_kernel(tile_h, zone_h, tide_h, depth_h, back_h, graz_h, quality_h, valid_h, row_h, col_h, out,
                tile, zone, tide, depth, back, graz, quality, valid, row, col, cell, seen, sems):
    pings = depth.shape[0]
    copies = [
        pltpu.make_async_copy(source, target, sems.at[i])
        for i, (source, target) in enumerate(
            (
                (tile_h, tile),
                (zone_h, zone),
                (tide_h, tide),
                (quality_h, quality),
                (valid_h, valid),
                (row_h, row),
                (col_h, col),
                (depth_h, depth),
                (back_h, back),
                (graz_h, graz),
            )
        )
    ]
    for copy in copies:
        copy.start()

    def empty(i, _):
        out[i, FIELDS - 1] = jnp.full((GROUPS, LANES), -1.0, F32)
        return 0

    lax.fori_loop(0, out.shape[0], empty, 0, unroll=8)

    def clear(i, _):
        seen[i] = 0
        return 0

    lax.fori_loop(0, seen.shape[0], clear, 0, unroll=8)
    for copy in copies:
        copy.wait()
    quality[...] = quality[...] * valid[...].astype(F32)
    cell[...] = (row[...] * TILE + col[...]).astype(F32)

    def place(p, _):
        target = tile[p]
        rank = seen[target]
        seen[target] = rank + 1
        down, across = lax.shift_right_logical(target, 4), target & 15
        chip = lax.shift_right_logical(down, 1) * 16 + across
        slot = chip * 4 + (down & 1) * 2 + rank
        offset = tide[zone[p]]
        here = pl.ds(p, 1)
        for f, field in enumerate((depth, back, graz, quality, cell)):
            values = offset - field[here, :] if f == 0 else field[here, :]
            for j in range(GROUPS):
                out[slot, f, pl.ds(j, 1), :] = values[:, j * LANES : (j + 1) * LANES]
        return 0

    lax.fori_loop(0, pings, place, 0, unroll=8)


def both(rows):
    return jnp.concatenate([rows, rows], 0).astype(BF16)


def factors(x, slot, spots):
    sub = lax.broadcasted_iota(jnp.int32, (8, LANES), 0)
    zero = jnp.zeros((16, LANES), BF16)
    one = jnp.ones((16, LANES), BF16)
    left, right = [], []
    for j in range(GROUPS):
        height, back, graz, weight, cell = (
            jnp.broadcast_to(x[slot, f, pl.ds(j, 1), :], (8, LANES)) for f in range(FIELDS)
        )
        first = jnp.where(
            (sub == 1) | (sub == 2) | (sub == 5),
            height,
            jnp.where((sub == 3) | (sub == 4), back, jnp.where(sub >= 6, graz, 1.0)),
        )
        second = jnp.where(
            sub == 2,
            height,
            jnp.where((sub == 4) | (sub == 5), back, jnp.where(sub == 7, graz, 1.0)),
        )
        stats = weight * first * second
        high = stats.astype(BF16).astype(F32)
        halves = jnp.concatenate([high, stats - high], 0).astype(BF16)
        coarse = jnp.floor(cell * (1.0 / 256.0))
        fine = both(cell - 256.0 * coarse)
        coarse = both(coarse)
        left.append(
            jnp.concatenate(
                [jnp.where(coarse == jnp.asarray(r, BF16), halves, zero) for r in range(16)], 0
            )
        )
        right.append(jnp.concatenate([jnp.where(fine == s, one, zero) for s in spots], 0))
    return jnp.concatenate(left, 1), jnp.concatenate(right, 1)


def deposit_kernel(x, mine, mates, acc, part, heads, table_v, table, sem):
    slots = x.shape[0]
    core = lax.axis_index("ty") % 2

    def head(s, _):
        heads[pl.ds(s, 1), :] = x[s, FIELDS - 1, pl.ds(0, 1), :]
        return 0

    lax.fori_loop(0, slots, head, 0, unroll=16)
    lane = lax.broadcasted_iota(jnp.int32, (8, slots), 1)
    pick = jnp.where(lax.broadcasted_iota(jnp.int32, (8, LANES), 1) == 0, 1.0, 0.0)
    filled = jnp.where(heads[...] >= 0.0, 1.0, 0.0)
    full = lax.dot_general(
        pick.astype(BF16), filled.astype(BF16), (((1,), (1,)), ((), ())),
        preferred_element_type=F32,
    )
    i = lax.broadcasted_iota(jnp.int32, (slots, slots), 0)
    j = lax.broadcasted_iota(jnp.int32, (slots, slots), 1)
    before = jnp.where((i < j) & ((i & 2) == (j & 2)), 1.0, 0.0).astype(BF16)
    position = jnp.dot(full.astype(BF16), before, preferred_element_type=F32)
    numbers = jnp.concatenate([lane.astype(F32), jnp.ones((8, slots), F32)], 0).astype(BF16)
    wanted = i.astype(F32)
    for side in range(2):
        ours = (lane & 2) == 2 * side
        key = jnp.where(ours & (full > 0.0), position, -1.0)
        match = jnp.where(jnp.broadcast_to(key[0:1], (slots, slots)) == wanted, 1.0, 0.0)
        found = lax.dot_general(
            numbers, match.astype(BF16), (((1,), (1,)), ((), ())), preferred_element_type=F32
        )
        gap = jnp.max(
            jnp.where(ours & (full == 0.0), lane.astype(F32), -1.0), axis=1, keepdims=True
        )
        count = jnp.sum(found[8:], axis=1, keepdims=True)
        listed = found[:8] + (1.0 - found[8:]) * gap
        table_v[side] = jnp.where(lane == slots - 1, count, listed).astype(jnp.int32)
    copy = pltpu.make_async_copy(table_v, table, sem)
    copy.start()
    acc[...] = jnp.zeros_like(acc)
    base = lax.broadcasted_iota(jnp.int32, (16, LANES), 0)
    spots = [(base + 16 * k).astype(F32).astype(BF16) for k in range(16)]
    copy.wait()
    counts = [table[side, 0, slots - 1] for side in range(2)]

    def add(first, side, size):
        pairs = [factors(x, table[side, 0, first + u], spots) for u in range(size)]
        left = jnp.concatenate([a for a, _ in pairs], 1)
        right = jnp.concatenate([b for _, b in pairs], 1)
        total = lax.dot_general(
            left, right, (((1,), (1,)), ((), ())), preferred_element_type=F32
        )
        acc[side, 0] += total[:, :LANES]
        acc[side, 1] += total[:, LANES:]

    whole = [(count + TAIL - 1) // BATCH for count in counts]
    rest = [
        (jnp.maximum(count - BATCH * n, 0) + TAIL - 1) // TAIL for count, n in zip(counts, whole)
    ]

    def step(t, _):
        side = (t >= whole[0]).astype(jnp.int32)
        add((t - side * whole[0]) * BATCH, side, BATCH)
        return 0

    def tail(t, _):
        side = (t >= rest[0]).astype(jnp.int32)
        start = jnp.where(side > 0, whole[1], whole[0]) * BATCH
        add(start + (t - side * rest[0]) * TAIL, side, TAIL)
        return 0

    lax.fori_loop(0, whole[0] + whole[1], step, 0)
    lax.fori_loop(0, rest[0] + rest[1], tail, 0)
    for side in range(2):
        for ch in range(CHANNELS):
            for piece in range(2):
                rows = acc[side, piece, pl.ds(ch, 16, stride=16), :]
                rows += acc[side, piece, pl.ds(ch + 8, 16, stride=16), :]
                for q in range(2):
                    part[ch, pl.ds(TILE * side + 2 * piece + q, 16, stride=4), 0:TILE] = rows[
                        :, q * TILE : (q + 1) * TILE
                    ]
    own = pl.ds(pl.multiple_of(core * (TILE - 8), 8), TILE + 8)
    other = pl.ds(pl.multiple_of((1 - core) * (TILE - 8), 8), TILE + 8)
    for ch in range(CHANNELS):
        mine[ch] = part[ch, own, 0:TILE]
        mates[ch] = part[ch, other, 0:TILE]


def join_kernel(mine, mates, total, rim):
    core = lax.axis_index("ty") % 2
    for ch in range(CHANNELS):
        total[ch] = mine[ch] + mates[ch]
        rim[ch] = total[ch, pl.ds(pl.multiple_of(core * TILE, 8), 8), :]


def smoothed(ext, ch):
    total = None
    for j in range(2 * MARGIN + 1):
        term = TAPS[j] * ext[ch, pl.ds(1 + j, TILE), :]
        total = term if total is None else total + term
    return total


def rows_kernel(window, rim, out, near, far, ext):
    place = lax.axis_index("ty")
    core = place % 2
    beyond = (place == 0) | (place == lax.axis_size("ty") - 1)
    odd = lax.axis_index("tx") % 2
    inside = pl.ds(pl.multiple_of(8 - core * 8, 8), TILE + 8)
    outside = pl.ds(pl.multiple_of(core * (TILE + 8), 8), 8)
    for ch in range(CHANNELS):
        ext[ch, inside, :] = window[ch]
        ext[ch, outside, :] = jnp.where(beyond, 0.0, rim[ch])
    for ch in range(CHANNELS):
        out[ch] = smoothed(ext, ch).T
        near[ch] = out[ch, pl.ds(pl.multiple_of((1 - odd) * (TILE - 8), 8), 8), :]
        far[ch] = out[ch, pl.ds(pl.multiple_of(odd * (TILE - 8), 8), 8), :]


def inner_kernel(own, out, ext):
    for ch in range(CHANNELS):
        ext[ch, 0:8, :] = jnp.zeros((8, TILE), F32)
        ext[ch, 8 : 8 + TILE, :] = own[ch]
        ext[ch, 8 + TILE : 16 + TILE, :] = jnp.zeros((8, TILE), F32)
    for ch in range(CHANNELS):
        out[ch] = smoothed(ext, ch)


def columns_kernel(own, inner, near, far, out, ext):
    place = lax.axis_index("tx")
    odd = place % 2
    beyond = (place == 0) | (place == lax.axis_size("tx") - 1)
    near_rows = pl.ds(pl.multiple_of((1 - odd) * 40, 8), 8)
    far_rows = pl.ds(pl.multiple_of(odd * 40, 8), 8)
    for ch in range(CHANNELS):
        ext[ch, 8:24, :] = own[ch, 0:16]
        ext[ch, 24:40, :] = own[ch, TILE - 16 : TILE]
        ext[ch, near_rows, :] = near[ch]
        ext[ch, far_rows, :] = jnp.where(beyond, 0.0, far[ch])
    scale = None
    for ch in range(CHANNELS):
        ends = []
        for first in (1, 25):
            total = None
            for j in range(2 * MARGIN + 1):
                term = TAPS[j] * ext[ch, pl.ds(first + j, 8), :]
                total = term if total is None else total + term
            ends.append(total)
        total = jnp.concatenate([ends[0], inner[ch, 8 : TILE - 8], ends[1]], 0)
        if ch == 0:
            scale = 1.0 + total
        out[ch] = (total / scale).T


def swap(x, axis, first):
    count = lax.axis_size(axis)
    pairs = [(i, (i + 1) % count) for i in range(first, count, 2)]
    return lax.ppermute(x, axis, pairs + [(b, a) for a, b in pairs])


def shards(depth, back, graz, quality, valid, row, col, zone, tile, tide):
    down, across = lax.axis_size("ty"), lax.axis_size("tx")
    slots = down * across * RANKS
    pings = depth.shape[0]
    shape = jax.ShapeDtypeStruct
    hbm = pl.BlockSpec(memory_space=pltpu.HBM)
    block = (pings, BEAMS)
    packed = pl.pallas_call(
        pack_kernel,
        out_shape=pltpu.VMEM((slots, FIELDS, GROUPS, LANES), F32),
        in_specs=[hbm] * 10,
        out_specs=vmem(),
        scratch_shapes=[
            pltpu.SMEM((pings,), jnp.int32),
            pltpu.SMEM((pings,), jnp.int32),
            pltpu.SMEM(tide.shape, F32),
        ]
        + [pltpu.VMEM(block, F32)] * 4
        + [pltpu.VMEM(block, jnp.int32)] * 3
        + [
            pltpu.VMEM(block, F32),
            pltpu.SMEM((down * across,), jnp.int32),
            pltpu.SemaphoreType.DMA((10,)),
        ],
        compiler_params=pltpu.CompilerParams(vmem_limit_bytes=60 * 2**20),
        name="pack",
    )(tile, zone, tide, depth, back, graz, quality, valid, row, col)
    groups = [
        [(2 * chip + core) * across + i for chip in range(down // 2) for i in range(across)]
        for core in range(2)
    ]
    arrived = lax.all_to_all(
        packed, ("ty", "tx"), split_axis=0, concat_axis=0, tiled=True, axis_index_groups=groups
    )
    window = shape((CHANNELS, TILE + 8, TILE), F32)
    rim = shape((CHANNELS, 8, TILE), F32)
    ext = pltpu.VMEM((CHANNELS, TILE + 16, TILE), F32)
    mine, mates = pl.pallas_call(
        deposit_kernel,
        out_shape=(window, window),
        in_specs=[vmem()],
        out_specs=(vmem(),) * 2,
        scratch_shapes=[
            pltpu.VMEM((2, 2, 256, LANES), F32),
            pltpu.VMEM((CHANNELS, 2 * TILE, LANES), F32),
            pltpu.VMEM((slots, LANES), F32),
            pltpu.VMEM((2, 8, slots), jnp.int32),
            pltpu.SMEM((2, 8, slots), jnp.int32),
            pltpu.SemaphoreType.DMA,
        ],
        compiler_params=VMEM,
        name="deposit",
    )(arrived)
    total, edge = pl.pallas_call(
        join_kernel,
        out_shape=(window, rim),
        in_specs=[vmem()] * 2,
        out_specs=(vmem(),) * 2,
        compiler_params=VMEM,
        name="join",
    )(mine, swap(mates, "ty", 0))
    rows, near, far = pl.pallas_call(
        rows_kernel,
        out_shape=(shape((CHANNELS, TILE, TILE), F32), rim, rim),
        in_specs=[vmem()] * 2,
        out_specs=(vmem(),) * 3,
        scratch_shapes=[ext],
        compiler_params=VMEM,
        name="rows",
    )(total, swap(edge, "ty", 1))
    near, far = swap(near, "tx", 0), swap(far, "tx", 1)
    inner = pl.pallas_call(
        inner_kernel,
        out_shape=shape((CHANNELS, TILE, TILE), F32),
        in_specs=[vmem()],
        out_specs=vmem(),
        scratch_shapes=[ext],
        compiler_params=VMEM,
        cost_estimate=pl.CostEstimate(flops=10**7, bytes_accessed=10**6, transcendentals=0),
        name="inner",
    )(rows)
    return pl.pallas_call(
        columns_kernel,
        out_shape=shape((CHANNELS, TILE, TILE), F32),
        in_specs=[vmem()] * 4,
        out_specs=vmem(),
        scratch_shapes=[pltpu.VMEM((CHANNELS, 48, TILE), F32)],
        compiler_params=VMEM,
        name="columns",
    )(rows, inner, near, far)


def solution(mesh):
    pings = P(("ty", "tx"))
    return jax.shard_map(
        shards,
        mesh=mesh,
        in_specs=(pings,) * 9 + (P(),),
        out_specs=P(None, "ty", "tx"),
        check_vma=False,
    )
```

```python
import functools
import math

import jax
import jax.numpy as jnp
from jax import lax
from jax.experimental import pallas as pl
from jax.experimental.pallas import tpu as pltpu
from jax.sharding import PartitionSpec as P

F32 = jnp.float32
BF16 = jnp.bfloat16
BEAMS = 512
CHANNELS = 8
MARGIN = 7
TILE = 64
FIELDS = 5
LANES = 128
GROUPS = BEAMS // LANES
RANKS = 2
BATCH = 32
TAIL = 8
SIGMA = 2.5
VMEM = pltpu.CompilerParams(vmem_limit_bytes=40 * 2**20)

_profile = [math.exp(-j * j / (2 * SIGMA * SIGMA)) for j in range(-MARGIN, MARGIN + 1)]
TAPS = [value / sum(_profile) for value in _profile]


def vmem():
    return pl.BlockSpec(memory_space=pltpu.VMEM)


def pack_kernel(tile_h, zone_h, tide_h, depth_h, back_h, graz_h, quality_h, valid_h, row_h, col_h, out,
                tile, zone, tide, depth, back, graz, quality, valid, row, col, cell, seen, sems):
    pings = depth.shape[0]
    copies = [
        pltpu.make_async_copy(source, target, sems.at[i])
        for i, (source, target) in enumerate(
            (
                (tile_h, tile),
                (zone_h, zone),
                (tide_h, tide),
                (quality_h, quality),
                (valid_h, valid),
                (row_h, row),
                (col_h, col),
                (depth_h, depth),
                (back_h, back),
                (graz_h, graz),
            )
        )
    ]
    for copy in copies:
        copy.start()

    def empty(i, _):
        out[i, FIELDS - 1] = jnp.full((GROUPS, LANES), -1.0, F32)
        return 0

    lax.fori_loop(0, out.shape[0], empty, 0, unroll=8)

    def clear(i, _):
        seen[i] = 0
        return 0

    lax.fori_loop(0, seen.shape[0], clear, 0, unroll=8)
    for copy in copies:
        copy.wait()
    quality[...] = quality[...] * valid[...].astype(F32)
    cell[...] = (row[...] * TILE + col[...]).astype(F32)

    def place(p, _):
        target = tile[p]
        rank = seen[target]
        seen[target] = rank + 1
        down, across = lax.shift_right_logical(target, 4), target & 15
        chip = lax.shift_right_logical(down, 1) * 16 + across
        slot = chip * 4 + (down & 1) * 2 + rank
        offset = tide[zone[p]]
        here = pl.ds(p, 1)
        for f, field in enumerate((depth, back, graz, quality, cell)):
            values = offset - field[here, :] if f == 0 else field[here, :]
            for j in range(GROUPS):
                out[slot, f, pl.ds(j, 1), :] = values[:, j * LANES : (j + 1) * LANES]
        return 0

    lax.fori_loop(0, pings, place, 0, unroll=8)


def both(rows):
    return jnp.concatenate([rows, rows], 0).astype(BF16)


def factors(x, slot, spots):
    sub = lax.broadcasted_iota(jnp.int32, (8, LANES), 0)
    zero = jnp.zeros((16, LANES), BF16)
    one = jnp.ones((16, LANES), BF16)
    left, right = [], []
    for j in range(GROUPS):
        height, back, graz, weight, cell = (
            jnp.broadcast_to(x[slot, f, pl.ds(j, 1), :], (8, LANES)) for f in range(FIELDS)
        )
        first = jnp.where(
            (sub == 1) | (sub == 2) | (sub == 5),
            height,
            jnp.where((sub == 3) | (sub == 4), back, jnp.where(sub >= 6, graz, 1.0)),
        )
        second = jnp.where(
            sub == 2,
            height,
            jnp.where((sub == 4) | (sub == 5), back, jnp.where(sub == 7, graz, 1.0)),
        )
        stats = weight * first * second
        high = stats.astype(BF16).astype(F32)
        halves = jnp.concatenate([high, stats - high], 0).astype(BF16)
        coarse = jnp.floor(cell * (1.0 / 256.0))
        fine = both(cell - 256.0 * coarse)
        coarse = both(coarse)
        left.append(
            jnp.concatenate(
                [jnp.where(coarse == jnp.asarray(r, BF16), halves, zero) for r in range(16)], 0
            )
        )
        right.append(jnp.concatenate([jnp.where(fine == s, one, zero) for s in spots], 0))
    return jnp.concatenate(left, 1), jnp.concatenate(right, 1)


def deposit_kernel(x, mine, mates, acc, part, heads, table_v, table, sem):
    slots = x.shape[0]
    core = lax.axis_index("ty") % 2

    def head(s, _):
        heads[pl.ds(s, 1), :] = x[s, FIELDS - 1, pl.ds(0, 1), :]
        return 0

    lax.fori_loop(0, slots, head, 0, unroll=16)
    lane = lax.broadcasted_iota(jnp.int32, (8, slots), 1)
    pick = jnp.where(lax.broadcasted_iota(jnp.int32, (8, LANES), 1) == 0, 1.0, 0.0)
    filled = jnp.where(heads[...] >= 0.0, 1.0, 0.0)
    full = lax.dot_general(
        pick.astype(BF16), filled.astype(BF16), (((1,), (1,)), ((), ())),
        preferred_element_type=F32,
    )
    i = lax.broadcasted_iota(jnp.int32, (slots, slots), 0)
    j = lax.broadcasted_iota(jnp.int32, (slots, slots), 1)
    before = jnp.where((i < j) & ((i & 2) == (j & 2)), 1.0, 0.0).astype(BF16)
    position = jnp.dot(full.astype(BF16), before, preferred_element_type=F32)
    numbers = jnp.concatenate([lane.astype(F32), jnp.ones((8, slots), F32)], 0).astype(BF16)
    wanted = i.astype(F32)
    for side in range(2):
        ours = (lane & 2) == 2 * side
        key = jnp.where(ours & (full > 0.0), position, -1.0)
        match = jnp.where(jnp.broadcast_to(key[0:1], (slots, slots)) == wanted, 1.0, 0.0)
        found = lax.dot_general(
            numbers, match.astype(BF16), (((1,), (1,)), ((), ())), preferred_element_type=F32
        )
        gap = jnp.max(
            jnp.where(ours & (full == 0.0), lane.astype(F32), -1.0), axis=1, keepdims=True
        )
        count = jnp.sum(found[8:], axis=1, keepdims=True)
        listed = found[:8] + (1.0 - found[8:]) * gap
        table_v[side : side + 1] = jnp.where(lane == slots - 1, count, listed)[0:1].astype(jnp.int32)
    copy = pltpu.make_async_copy(table_v.at[0:2], table, sem)
    copy.start()
    acc[...] = jnp.zeros_like(acc)
    base = lax.broadcasted_iota(jnp.int32, (16, LANES), 0)
    spots = [(base + 16 * k).astype(F32).astype(BF16) for k in range(16)]
    copy.wait()
    counts = [table[side, slots - 1] for side in range(2)]

    def add(first, side, size):
        pairs = [factors(x, table[side, first + u], spots) for u in range(size)]
        left = jnp.concatenate([a for a, _ in pairs], 1)
        right = jnp.concatenate([b for _, b in pairs], 1)
        total = lax.dot_general(
            left, right, (((1,), (1,)), ((), ())), preferred_element_type=F32
        )
        acc[side, 0] += total[:, :LANES]
        acc[side, 1] += total[:, LANES:]

    whole = [(count + TAIL - 1) // BATCH for count in counts]
    rest = [
        (jnp.maximum(count - BATCH * n, 0) + TAIL - 1) // TAIL for count, n in zip(counts, whole)
    ]

    def step(t, _):
        side = (t >= whole[0]).astype(jnp.int32)
        add((t - side * whole[0]) * BATCH, side, BATCH)
        return 0

    def tail(t, _):
        side = (t >= rest[0]).astype(jnp.int32)
        start = jnp.where(side > 0, whole[1], whole[0]) * BATCH
        add(start + (t - side * rest[0]) * TAIL, side, TAIL)
        return 0

    lax.fori_loop(0, whole[0] + whole[1], step, 0)
    lax.fori_loop(0, rest[0] + rest[1], tail, 0)
    for side in range(2):
        for ch in range(CHANNELS):
            for piece in range(2):
                rows = acc[side, piece, pl.ds(ch, 16, stride=16), :]
                rows += acc[side, piece, pl.ds(ch + 8, 16, stride=16), :]
                for q in range(2):
                    part[ch, pl.ds(TILE * side + 2 * piece + q, 16, stride=4), 0:TILE] = rows[
                        :, q * TILE : (q + 1) * TILE
                    ]
    own = pl.ds(pl.multiple_of(core * (TILE - 8), 8), TILE + 8)
    other = pl.ds(pl.multiple_of((1 - core) * (TILE - 8), 8), TILE + 8)
    for ch in range(CHANNELS):
        mine[ch] = part[ch, own, 0:TILE]
        mates[ch] = part[ch, other, 0:TILE]


def join_kernel(mine, mates, total, rim):
    core = lax.axis_index("ty") % 2
    for ch in range(CHANNELS):
        total[ch] = mine[ch] + mates[ch]
        rim[ch] = total[ch, pl.ds(pl.multiple_of(core * TILE, 8), 8), :]


def smoothed(ext, ch):
    total = None
    for j in range(2 * MARGIN + 1):
        term = TAPS[j] * ext[ch, pl.ds(1 + j, TILE), :]
        total = term if total is None else total + term
    return total


def rows_kernel(window, rim, out, near, far, ext):
    place = lax.axis_index("ty")
    core = place % 2
    beyond = (place == 0) | (place == lax.axis_size("ty") - 1)
    odd = lax.axis_index("tx") % 2
    inside = pl.ds(pl.multiple_of(8 - core * 8, 8), TILE + 8)
    outside = pl.ds(pl.multiple_of(core * (TILE + 8), 8), 8)
    for ch in range(CHANNELS):
        ext[ch, inside, :] = window[ch]
        ext[ch, outside, :] = jnp.where(beyond, 0.0, rim[ch])
    for ch in range(CHANNELS):
        out[ch] = smoothed(ext, ch).T
        near[ch] = out[ch, pl.ds(pl.multiple_of((1 - odd) * (TILE - 8), 8), 8), :]
        far[ch] = out[ch, pl.ds(pl.multiple_of(odd * (TILE - 8), 8), 8), :]


def inner_kernel(own, out, ext):
    for ch in range(CHANNELS):
        ext[ch, 0:8, :] = jnp.zeros((8, TILE), F32)
        ext[ch, 8 : 8 + TILE, :] = own[ch]
        ext[ch, 8 + TILE : 16 + TILE, :] = jnp.zeros((8, TILE), F32)
    for ch in range(CHANNELS):
        out[ch] = smoothed(ext, ch)


def columns_kernel(own, inner, near, far, out, ext):
    place = lax.axis_index("tx")
    odd = place % 2
    beyond = (place == 0) | (place == lax.axis_size("tx") - 1)
    near_rows = pl.ds(pl.multiple_of((1 - odd) * 40, 8), 8)
    far_rows = pl.ds(pl.multiple_of(odd * 40, 8), 8)
    for ch in range(CHANNELS):
        ext[ch, 8:24, :] = own[ch, 0:16]
        ext[ch, 24:40, :] = own[ch, TILE - 16 : TILE]
        ext[ch, near_rows, :] = near[ch]
        ext[ch, far_rows, :] = jnp.where(beyond, 0.0, far[ch])
    scale = None
    for ch in range(CHANNELS):
        ends = []
        for first in (1, 25):
            total = None
            for j in range(2 * MARGIN + 1):
                term = TAPS[j] * ext[ch, pl.ds(first + j, 8), :]
                total = term if total is None else total + term
            ends.append(total)
        total = jnp.concatenate([ends[0], inner[ch, 8 : TILE - 8], ends[1]], 0)
        if ch == 0:
            scale = 1.0 + total
        out[ch] = (total / scale).T


def swap(x, axis, first):
    count = lax.axis_size(axis)
    pairs = [(i, (i + 1) % count) for i in range(first, count, 2)]
    return lax.ppermute(x, axis, pairs + [(b, a) for a, b in pairs])


def shards(depth, back, graz, quality, valid, row, col, zone, tile, tide):
    down, across = lax.axis_size("ty"), lax.axis_size("tx")
    slots = down * across * RANKS
    pings = depth.shape[0]
    shape = jax.ShapeDtypeStruct
    hbm = pl.BlockSpec(memory_space=pltpu.HBM)
    block = (pings, BEAMS)
    packed = pl.pallas_call(
        pack_kernel,
        out_shape=pltpu.VMEM((slots, FIELDS, GROUPS, LANES), F32),
        in_specs=[hbm] * 10,
        out_specs=vmem(),
        scratch_shapes=[
            pltpu.SMEM((pings,), jnp.int32),
            pltpu.SMEM((pings,), jnp.int32),
            pltpu.SMEM(tide.shape, F32),
        ]
        + [pltpu.VMEM(block, F32)] * 4
        + [pltpu.VMEM(block, jnp.int32)] * 3
        + [
            pltpu.VMEM(block, F32),
            pltpu.SMEM((down * across,), jnp.int32),
            pltpu.SemaphoreType.DMA((10,)),
        ],
        compiler_params=pltpu.CompilerParams(vmem_limit_bytes=60 * 2**20),
        name="pack",
    )(tile, zone, tide, depth, back, graz, quality, valid, row, col)
    groups = [
        [(2 * chip + core) * across + i for chip in range(down // 2) for i in range(across)]
        for core in range(2)
    ]
    arrived = lax.all_to_all(
        packed, ("ty", "tx"), split_axis=0, concat_axis=0, tiled=True, axis_index_groups=groups
    )
    window = shape((CHANNELS, TILE + 8, TILE), F32)
    rim = shape((CHANNELS, 8, TILE), F32)
    ext = pltpu.VMEM((CHANNELS, TILE + 16, TILE), F32)
    mine, mates = pl.pallas_call(
        deposit_kernel,
        out_shape=(window, window),
        in_specs=[vmem()],
        out_specs=(vmem(),) * 2,
        scratch_shapes=[
            pltpu.VMEM((2, 2, 256, LANES), F32),
            pltpu.VMEM((CHANNELS, 2 * TILE, LANES), F32),
            pltpu.VMEM((slots, LANES), F32),
            pltpu.VMEM((8, slots), jnp.int32),
            pltpu.SMEM((2, slots), jnp.int32),
            pltpu.SemaphoreType.DMA,
        ],
        compiler_params=VMEM,
        name="deposit",
    )(arrived)
    total, edge = pl.pallas_call(
        join_kernel,
        out_shape=(window, rim),
        in_specs=[vmem()] * 2,
        out_specs=(vmem(),) * 2,
        compiler_params=VMEM,
        name="join",
    )(mine, swap(mates, "ty", 0))
    rows, near, far = pl.pallas_call(
        rows_kernel,
        out_shape=(shape((CHANNELS, TILE, TILE), F32), rim, rim),
        in_specs=[vmem()] * 2,
        out_specs=(vmem(),) * 3,
        scratch_shapes=[ext],
        compiler_params=VMEM,
        name="rows",
    )(total, swap(edge, "ty", 1))
    near, far = swap(near, "tx", 0), swap(far, "tx", 1)
    inner = pl.pallas_call(
        inner_kernel,
        out_shape=shape((CHANNELS, TILE, TILE), F32),
        in_specs=[vmem()],
        out_specs=vmem(),
        scratch_shapes=[ext],
        compiler_params=VMEM,
        cost_estimate=pl.CostEstimate(flops=10**7, bytes_accessed=10**6, transcendentals=0),
        name="inner",
    )(rows)
    return pl.pallas_call(
        columns_kernel,
        out_shape=shape((CHANNELS, TILE, TILE), F32),
        in_specs=[vmem()] * 4,
        out_specs=vmem(),
        scratch_shapes=[pltpu.VMEM((CHANNELS, 48, TILE), F32)],
        compiler_params=VMEM,
        name="columns",
    )(rows, inner, near, far)


def solution(mesh):
    pings = P(("ty", "tx"))
    return jax.shard_map(
        shards,
        mesh=mesh,
        in_specs=(pings,) * 9 + (P(),),
        out_specs=P(None, "ty", "tx"),
        check_vma=False,
    )
```

```python
import functools
import math

import jax
import jax.numpy as jnp
from jax import lax
from jax.experimental import pallas as pl
from jax.experimental.pallas import tpu as pltpu
from jax.sharding import PartitionSpec as P

F32 = jnp.float32
BF16 = jnp.bfloat16
BEAMS = 512
CHANNELS = 8
MARGIN = 7
TILE = 64
FIELDS = 5
LANES = 128
GROUPS = BEAMS // LANES
RANKS = 2
BATCH = 32
TAIL = 8
SIGMA = 2.5
VMEM = pltpu.CompilerParams(vmem_limit_bytes=40 * 2**20)

_profile = [math.exp(-j * j / (2 * SIGMA * SIGMA)) for j in range(-MARGIN, MARGIN + 1)]
TAPS = [value / sum(_profile) for value in _profile]


def vmem():
    return pl.BlockSpec(memory_space=pltpu.VMEM)


def pack_kernel(tile_h, zone_h, tide_h, depth_h, back_h, graz_h, quality_h, valid_h, row_h, col_h, out,
                tile, zone, tide, depth, back, graz, quality, valid, row, col, cell, seen, sems):
    pings = depth.shape[0]
    copies = [
        pltpu.make_async_copy(source, target, sems.at[i])
        for i, (source, target) in enumerate(
            (
                (tile_h, tile),
                (zone_h, zone),
                (tide_h, tide),
                (quality_h, quality),
                (valid_h, valid),
                (row_h, row),
                (col_h, col),
                (depth_h, depth),
                (back_h, back),
                (graz_h, graz),
            )
        )
    ]
    for copy in copies:
        copy.start()

    def empty(i, _):
        out[i, FIELDS - 1] = jnp.full((GROUPS, LANES), -1.0, F32)
        return 0

    lax.fori_loop(0, out.shape[0], empty, 0, unroll=8)

    def clear(i, _):
        seen[i] = 0
        return 0

    lax.fori_loop(0, seen.shape[0], clear, 0, unroll=8)
    for copy in copies:
        copy.wait()
    quality[...] = quality[...] * valid[...].astype(F32)
    cell[...] = (row[...] * TILE + col[...]).astype(F32)

    def place(p, _):
        target = tile[p]
        rank = seen[target]
        seen[target] = rank + 1
        down, across = lax.shift_right_logical(target, 4), target & 15
        chip = lax.shift_right_logical(down, 1) * 16 + across
        slot = chip * 4 + (down & 1) * 2 + rank
        offset = tide[zone[p]]
        here = pl.ds(p, 1)
        for f, field in enumerate((depth, back, graz, quality, cell)):
            values = offset - field[here, :] if f == 0 else field[here, :]
            for j in range(GROUPS):
                out[slot, f, pl.ds(j, 1), :] = values[:, j * LANES : (j + 1) * LANES]
        return 0

    lax.fori_loop(0, pings, place, 0, unroll=8)


def both(rows):
    return jnp.concatenate([rows, rows], 0).astype(BF16)


def factors(x, slot, spots):
    sub = lax.broadcasted_iota(jnp.int32, (8, LANES), 0)
    zero = jnp.zeros((16, LANES), BF16)
    one = jnp.ones((16, LANES), BF16)
    left, right = [], []
    for j in range(GROUPS):
        height, back, graz, weight, cell = (
            jnp.broadcast_to(x[slot, f, pl.ds(j, 1), :], (8, LANES)) for f in range(FIELDS)
        )
        first = jnp.where(
            (sub == 1) | (sub == 2) | (sub == 5),
            height,
            jnp.where((sub == 3) | (sub == 4), back, jnp.where(sub >= 6, graz, 1.0)),
        )
        second = jnp.where(
            sub == 2,
            height,
            jnp.where((sub == 4) | (sub == 5), back, jnp.where(sub == 7, graz, 1.0)),
        )
        stats = weight * first * second
        high = stats.astype(BF16).astype(F32)
        halves = jnp.concatenate([high, stats - high], 0).astype(BF16)
        coarse = jnp.floor(cell * (1.0 / 256.0))
        fine = both(cell - 256.0 * coarse)
        coarse = both(coarse)
        left.append(
            jnp.concatenate(
                [jnp.where(coarse == jnp.asarray(r, BF16), halves, zero) for r in range(16)], 0
            )
        )
        right.append(jnp.concatenate([jnp.where(fine == s, one, zero) for s in spots], 0))
    return jnp.concatenate(left, 1), jnp.concatenate(right, 1)


def deposit_kernel(x, mine, mates, acc, part, heads, table_v, table, sem):
    slots = x.shape[0]
    core = lax.axis_index("ty") % 2

    def head(s, _):
        heads[pl.ds(s, 1), :] = x[s, FIELDS - 1, pl.ds(0, 1), :]
        return 0

    lax.fori_loop(0, slots, head, 0, unroll=16)
    lane = lax.broadcasted_iota(jnp.int32, (8, slots), 1)
    pick = jnp.where(lax.broadcasted_iota(jnp.int32, (8, LANES), 1) == 0, 1.0, 0.0)
    filled = jnp.where(heads[...] >= 0.0, 1.0, 0.0)
    full = lax.dot_general(
        pick.astype(BF16), filled.astype(BF16), (((1,), (1,)), ((), ())),
        preferred_element_type=F32,
    )
    i = lax.broadcasted_iota(jnp.int32, (slots, slots), 0)
    j = lax.broadcasted_iota(jnp.int32, (slots, slots), 1)
    before = jnp.where((i < j) & ((i & 2) == (j & 2)), 1.0, 0.0).astype(BF16)
    position = jnp.dot(full.astype(BF16), before, preferred_element_type=F32)
    numbers = jnp.concatenate([lane.astype(F32), jnp.ones((8, slots), F32)], 0).astype(BF16)
    wanted = i.astype(F32)
    for side in range(2):
        ours = (lane & 2) == 2 * side
        key = jnp.where(ours & (full > 0.0), position, -1.0)
        match = jnp.where(jnp.broadcast_to(key[0:1], (slots, slots)) == wanted, 1.0, 0.0)
        found = lax.dot_general(
            numbers, match.astype(BF16), (((1,), (1,)), ((), ())), preferred_element_type=F32
        )
        gap = jnp.max(
            jnp.where(ours & (full == 0.0), lane.astype(F32), -1.0), axis=1, keepdims=True
        )
        count = jnp.sum(found[8:], axis=1, keepdims=True)
        listed = found[:8] + (1.0 - found[8:]) * gap
        table_v[side : side + 1] = jnp.where(lane == slots - 1, count, listed)[0:1].astype(jnp.int32)
    copy = pltpu.make_async_copy(table_v.at[0:2], table, sem)
    copy.start()
    acc[...] = jnp.zeros_like(acc)
    base = lax.broadcasted_iota(jnp.int32, (16, LANES), 0)
    spots = [(base + 16 * k).astype(F32).astype(BF16) for k in range(16)]
    copy.wait()
    counts = [table[side, slots - 1] for side in range(2)]

    def add(first, side, size):
        pairs = [factors(x, table[side, first + u], spots) for u in range(size)]
        left = jnp.concatenate([a for a, _ in pairs], 1)
        right = jnp.concatenate([b for _, b in pairs], 1)
        total = lax.dot_general(
            left, right, (((1,), (1,)), ((), ())), preferred_element_type=F32
        )
        acc[side, 0] += total[:, :LANES]
        acc[side, 1] += total[:, LANES:]

    whole = [(count + TAIL - 1) // BATCH for count in counts]
    rest = [
        (jnp.maximum(count - BATCH * n, 0) + TAIL - 1) // TAIL for count, n in zip(counts, whole)
    ]

    def step(t, _):
        side = (t >= whole[0]).astype(jnp.int32)
        add((t - side * whole[0]) * BATCH, side, BATCH)
        return 0

    def tail(t, _):
        side = (t >= rest[0]).astype(jnp.int32)
        start = jnp.where(side > 0, whole[1], whole[0]) * BATCH
        add(start + (t - side * rest[0]) * TAIL, side, TAIL)
        return 0

    lax.fori_loop(0, whole[0] + whole[1], step, 0)
    lax.fori_loop(0, rest[0] + rest[1], tail, 0)
    for side in range(2):
        for ch in range(CHANNELS):
            for piece in range(2):
                rows = acc[side, piece, pl.ds(ch, 16, stride=16), :]
                rows += acc[side, piece, pl.ds(ch + 8, 16, stride=16), :]
                for q in range(2):
                    part[ch, pl.ds(TILE * side + 2 * piece + q, 16, stride=4), 0:TILE] = rows[
                        :, q * TILE : (q + 1) * TILE
                    ]
    own = pl.ds(pl.multiple_of(core * (TILE - 8), 8), TILE + 8)
    other = pl.ds(pl.multiple_of((1 - core) * (TILE - 8), 8), TILE + 8)
    for ch in range(CHANNELS):
        mine[ch] = part[ch, own, 0:TILE]
        mates[ch] = part[ch, other, 0:TILE]


def join_kernel(mine, mates, total, rim):
    core = lax.axis_index("ty") % 2
    for ch in range(CHANNELS):
        total[ch] = mine[ch] + mates[ch]
        rim[ch] = total[ch, pl.ds(pl.multiple_of(core * TILE, 8), 8), :]


def smoothed(ext, ch):
    total = None
    for j in range(2 * MARGIN + 1):
        term = TAPS[j] * ext[ch, pl.ds(1 + j, TILE), :]
        total = term if total is None else total + term
    return total


def inner_rows_kernel(window, out, ext):
    core = lax.axis_index("ty") % 2
    inside = pl.ds(pl.multiple_of(8 - core * 8, 8), TILE + 8)
    outside = pl.ds(pl.multiple_of(core * (TILE + 8), 8), 8)
    for ch in range(CHANNELS):
        ext[ch, inside, :] = window[ch]
        ext[ch, outside, :] = jnp.zeros((8, TILE), F32)
    for ch in range(CHANNELS):
        out[ch] = smoothed(ext, ch)


def rows_kernel(window, inner, rim, out, near, far, ext, whole):
    place = lax.axis_index("ty")
    core = place % 2
    beyond = (place == 0) | (place == lax.axis_size("ty") - 1)
    odd = lax.axis_index("tx") % 2
    inside = pl.ds(pl.multiple_of(8 - core * 8, 8), 16)
    outside = pl.ds(pl.multiple_of(core * 16, 8), 8)
    outer = pl.ds(pl.multiple_of(core * (TILE - 8), 8), 8)
    last = pl.ds(pl.multiple_of(core * (TILE - 8), 8), 16)
    for ch in range(CHANNELS):
        ext[ch, inside, :] = window[ch, last, :]
        ext[ch, outside, :] = jnp.where(beyond, 0.0, rim[ch])
    for ch in range(CHANNELS):
        total = None
        for j in range(2 * MARGIN + 1):
            term = TAPS[j] * ext[ch, pl.ds(1 + j, 8), :]
            total = term if total is None else total + term
        whole[ch] = inner[ch]
        whole[ch, outer, :] = total
        out[ch] = whole[ch].T
        near[ch] = out[ch, pl.ds(pl.multiple_of((1 - odd) * (TILE - 8), 8), 8), :]
        far[ch] = out[ch, pl.ds(pl.multiple_of(odd * (TILE - 8), 8), 8), :]


def inner_kernel(own, out, ext):
    for ch in range(CHANNELS):
        ext[ch, 0:8, :] = jnp.zeros((8, TILE), F32)
        ext[ch, 8 : 8 + TILE, :] = own[ch]
        ext[ch, 8 + TILE : 16 + TILE, :] = jnp.zeros((8, TILE), F32)
    for ch in range(CHANNELS):
        out[ch] = smoothed(ext, ch)


def columns_kernel(own, inner, near, far, out, ext):
    place = lax.axis_index("tx")
    odd = place % 2
    beyond = (place == 0) | (place == lax.axis_size("tx") - 1)
    near_rows = pl.ds(pl.multiple_of((1 - odd) * 40, 8), 8)
    far_rows = pl.ds(pl.multiple_of(odd * 40, 8), 8)
    for ch in range(CHANNELS):
        ext[ch, 8:24, :] = own[ch, 0:16]
        ext[ch, 24:40, :] = own[ch, TILE - 16 : TILE]
        ext[ch, near_rows, :] = near[ch]
        ext[ch, far_rows, :] = jnp.where(beyond, 0.0, far[ch])
    scale = None
    for ch in range(CHANNELS):
        ends = []
        for first in (1, 25):
            total = None
            for j in range(2 * MARGIN + 1):
                term = TAPS[j] * ext[ch, pl.ds(first + j, 8), :]
                total = term if total is None else total + term
            ends.append(total)
        total = jnp.concatenate([ends[0], inner[ch, 8 : TILE - 8], ends[1]], 0)
        if ch == 0:
            scale = 1.0 + total
        out[ch] = (total / scale).T


def swap(x, axis, first):
    count = lax.axis_size(axis)
    pairs = [(i, (i + 1) % count) for i in range(first, count, 2)]
    return lax.ppermute(x, axis, pairs + [(b, a) for a, b in pairs])


def shards(depth, back, graz, quality, valid, row, col, zone, tile, tide):
    down, across = lax.axis_size("ty"), lax.axis_size("tx")
    slots = down * across * RANKS
    pings = depth.shape[0]
    shape = jax.ShapeDtypeStruct
    hbm = pl.BlockSpec(memory_space=pltpu.HBM)
    block = (pings, BEAMS)
    packed = pl.pallas_call(
        pack_kernel,
        out_shape=pltpu.VMEM((slots, FIELDS, GROUPS, LANES), F32),
        in_specs=[hbm] * 10,
        out_specs=vmem(),
        scratch_shapes=[
            pltpu.SMEM((pings,), jnp.int32),
            pltpu.SMEM((pings,), jnp.int32),
            pltpu.SMEM(tide.shape, F32),
        ]
        + [pltpu.VMEM(block, F32)] * 4
        + [pltpu.VMEM(block, jnp.int32)] * 3
        + [
            pltpu.VMEM(block, F32),
            pltpu.SMEM((down * across,), jnp.int32),
            pltpu.SemaphoreType.DMA((10,)),
        ],
        compiler_params=pltpu.CompilerParams(vmem_limit_bytes=60 * 2**20),
        name="pack",
    )(tile, zone, tide, depth, back, graz, quality, valid, row, col)
    groups = [
        [(2 * chip + core) * across + i for chip in range(down // 2) for i in range(across)]
        for core in range(2)
    ]
    arrived = lax.all_to_all(
        packed, ("ty", "tx"), split_axis=0, concat_axis=0, tiled=True, axis_index_groups=groups
    )
    window = shape((CHANNELS, TILE + 8, TILE), F32)
    rim = shape((CHANNELS, 8, TILE), F32)
    ext = pltpu.VMEM((CHANNELS, TILE + 16, TILE), F32)
    mine, mates = pl.pallas_call(
        deposit_kernel,
        out_shape=(window, window),
        in_specs=[vmem()],
        out_specs=(vmem(),) * 2,
        scratch_shapes=[
            pltpu.VMEM((2, 2, 256, LANES), F32),
            pltpu.VMEM((CHANNELS, 2 * TILE, LANES), F32),
            pltpu.VMEM((slots, LANES), F32),
            pltpu.VMEM((8, slots), jnp.int32),
            pltpu.SMEM((2, slots), jnp.int32),
            pltpu.SemaphoreType.DMA,
        ],
        compiler_params=VMEM,
        name="deposit",
    )(arrived)
    total, edge = pl.pallas_call(
        join_kernel,
        out_shape=(window, rim),
        in_specs=[vmem()] * 2,
        out_specs=(vmem(),) * 2,
        compiler_params=VMEM,
        name="join",
    )(mine, swap(mates, "ty", 0))
    square = shape((CHANNELS, TILE, TILE), F32)
    edge = swap(edge, "ty", 1)
    inner_rows = pl.pallas_call(
        inner_rows_kernel,
        out_shape=square,
        in_specs=[vmem()],
        out_specs=vmem(),
        scratch_shapes=[ext],
        compiler_params=VMEM,
        cost_estimate=pl.CostEstimate(flops=10**7, bytes_accessed=10**6, transcendentals=0),
        name="inner_rows",
    )(total)
    rows, near, far = pl.pallas_call(
        rows_kernel,
        out_shape=(square, rim, rim),
        in_specs=[vmem()] * 3,
        out_specs=(vmem(),) * 3,
        scratch_shapes=[
            pltpu.VMEM((CHANNELS, 24, TILE), F32),
            pltpu.VMEM((CHANNELS, TILE, TILE), F32),
        ],
        compiler_params=VMEM,
        name="rows",
    )(total, inner_rows, edge)
    near, far = swap(near, "tx", 0), swap(far, "tx", 1)
    inner = pl.pallas_call(
        inner_kernel,
        out_shape=shape((CHANNELS, TILE, TILE), F32),
        in_specs=[vmem()],
        out_specs=vmem(),
        scratch_shapes=[ext],
        compiler_params=VMEM,
        cost_estimate=pl.CostEstimate(flops=10**7, bytes_accessed=10**6, transcendentals=0),
        name="inner",
    )(rows)
    return pl.pallas_call(
        columns_kernel,
        out_shape=shape((CHANNELS, TILE, TILE), F32),
        in_specs=[vmem()] * 4,
        out_specs=vmem(),
        scratch_shapes=[pltpu.VMEM((CHANNELS, 48, TILE), F32)],
        compiler_params=VMEM,
        name="columns",
    )(rows, inner, near, far)


def solution(mesh):
    pings = P(("ty", "tx"))
    return jax.shard_map(
        shards,
        mesh=mesh,
        in_specs=(pings,) * 9 + (P(),),
        out_specs=P(None, "ty", "tx"),
        check_vma=False,
    )
```
